128 devices in a mesh: group: 4 (over z), fsdp: 32 (over x, y, core).
Axes of the slice: x: 4, y: 4, z: 4, core: 2. Of those that a mesh axis runs over, the one named last changes fastest.
Arguments:
- gradient: bfloat16 [8192, 8192], P('fsdp', 'group'), may hold values from -135 to 135
- second_moment: float32 [8192, 8192], P('fsdp', 'group'), may hold values from 0.05 to 5
- left_root: float32 [4, 32, 2, 1024, 1024], P('group', 'fsdp'), may hold values from -3 to 3, as said below
- right_root: float32 [4, 32, 2, 1024, 1024], P('group', 'fsdp'), may hold values from -3 to 3, as said below
- block_rows: int32 [4, 16], replicated, may hold values from 0 to 7, as said below
- block_cols: int32 [4, 16], replicated, may hold values from 0 to 1, as said below
- block_owner: int32 [4, 16], replicated, may hold values from 0 to 31, as said below
Outputs:
- update: bfloat16 [8192, 8192], P('fsdp')
- moment: float32 [8192, 8192], P('fsdp', 'group')
The draws below stay inside these ranges and needn't reach their ends.
Inputs may be any that keep to these rules, and one draw needn't show every extreme that they name: In each group, the pairs (block_rows, block_cols) over the list name every block of the 8 x 2 grid once. `block_cols`: see block_rows. `block_owner`: in each group a device owns at most 2 blocks, and exactly 2 for some device; a device owns at most one block of any block row and at most one of any block column. `left_root`: Symmetric. `right_root`: Symmetric.
All inputs are finite; a program needn't handle non-finite values.
Results may differ from the reference program's by a relative error of at most 0.001.
Values may be sent and summed in bfloat16 or wider, within the bound.
No kernel may reach another device: no remote copies, remote signals or barrier semaphores. Data moves between devices by JAX's collectives and lax.ppermute only.
A program may use at most 128 MiB of HBM per device.

```python
import math
import jax
import jax.numpy as jnp
from jax import lax

ROWS = 8192
BS = 1024
COLB = 2
MOST = 2
NBLK = 16
COLS = 8192
N_GROUP = 4
N_FSDP = 32


def block_table(key):
    row_total = ROWS // BS

    def one_group(group_key):
        first, second, third, fourth, fifth = jax.random.split(group_key, 5)
        modulus = jax.random.randint(first, (), row_total, N_FSDP + 1)
        offset = jax.random.randint(second, (), 1, row_total)
        devices = jax.random.permutation(third, N_FSDP).astype(jnp.int32)
        row_perm = jax.random.permutation(fourth, row_total).astype(jnp.int32)
        order = jax.random.permutation(fifth, NBLK).astype(jnp.int32)
        rows = (order // COLB).astype(jnp.int32)
        cols = (order % COLB).astype(jnp.int32)
        owners = devices[(row_perm[rows] + cols * offset) % modulus]
        return (rows, cols, owners.astype(jnp.int32))
    return jax.vmap(one_group)(jax.random.split(key, N_GROUP))


def draw_block_rows(key, part):
    shared = block_table(key)
    return shared[0]


def draw_block_cols(key, part):
    shared = block_table(key)
    return shared[1]


def draw_block_owner(key, part):
    shared = block_table(key)
    return shared[2]


def draw_gradient(key, part):
    key = jax.random.fold_in(key, 11)
    first, second, third = jax.random.split(key, 3)
    trend = 1.0 + 2.0 * jnp.arange(ROWS, dtype=jnp.float32) / ROWS
    row_scale = jnp.exp(jax.random.uniform(first, (ROWS,), jnp.float32, math.log(0.3), math.log(3.0))) * trend
    col_scale = jnp.exp(jax.random.uniform(second, (COLS,), jnp.float32, math.log(0.3), math.log(3.0)))
    values = jax.random.normal(third, (ROWS, COLS), jnp.float32)
    values = jnp.clip(values, -5.0, 5.0)
    return (values * row_scale[:, None] * col_scale[None, :]).astype(jnp.bfloat16)


def root_matrices(key, off_scale, diag_low, diag_high):
    first, second = jax.random.split(key)
    shape = (N_GROUP, N_FSDP, MOST, BS, BS)
    off = jnp.clip(jax.random.normal(first, shape, jnp.float32), -6.0, 6.0)
    off = off * (off_scale / math.sqrt(BS))
    symmetric = 0.5 * (off + jnp.swapaxes(off, -1, -2))
    diag = jnp.exp(jax.random.uniform(second, (N_GROUP, N_FSDP, MOST, BS), jnp.float32, math.log(diag_low), math.log(diag_high)))
    identity = jnp.eye(BS, dtype=jnp.float32)
    return symmetric + diag[..., :, None] * identity


def draw_left_root(key, part):
    key = jax.random.fold_in(key, 21)
    return root_matrices(key, 0.5, 0.5, 2.0)


def draw_right_root(key, part):
    key = jax.random.fold_in(key, 22)
    return root_matrices(key, 0.5, 0.5, 2.0)


def block_scale(rng, shape, cuts, smallest, high):
    gain, own = 1.0, jax.random.fold_in(rng, 6)
    for position, parts in cuts:
        draws = jnp.exp(jax.random.uniform(jax.random.fold_in(own, position), (parts,), jnp.float32, smallest / len(cuts), high / len(cuts)))
        gain = gain * jnp.repeat(draws, shape[position] // parts).reshape([-1 if axis == position else 1 for axis in range(len(shape))])
    return gain


def setup_inputs(seed: int = 0) -> dict:
    streams_of = jax.random.split(jax.random.key(seed), 8)
    return {
        "gradient": draw_gradient(jax.random.fold_in(streams_of[7], 71), 0),
        "second_moment": jnp.clip(jnp.exp(math.log(5.0) - 4.6051702 * jax.random.uniform(streams_of[1], (ROWS, COLS), jnp.float32) ** block_scale(streams_of[1], (ROWS, COLS), ((0, 32), (1, 4)), -0.2, 0.2)), 0.05, 5.0),
        "left_root": draw_left_root(jax.random.fold_in(streams_of[7], 71), 0),
        "right_root": draw_right_root(jax.random.fold_in(streams_of[7], 71), 0),
        "block_rows": draw_block_rows(jax.random.fold_in(streams_of[7], 71), 0),
        "block_cols": draw_block_cols(jax.random.fold_in(streams_of[7], 71), 0),
        "block_owner": draw_block_owner(jax.random.fold_in(streams_of[7], 71), 0),
    }


BETA_TWO = 0.999
ADAM_EPS = 1e-08
NORM_EPS = 1e-06

def reference(gradient, second_moment, left_root, right_root, block_rows, block_cols, block_owner):
    grad_float = gradient.astype(jnp.float32)
    moment = BETA_TWO * second_moment + (1.0 - BETA_TWO) * grad_float * grad_float
    adam_dir = grad_float / (jnp.sqrt(moment) + ADAM_EPS)
    positions = jnp.arange(NBLK, dtype=jnp.int32)
    earlier = positions[None, :] < positions[:, None]
    same_owner = block_owner[:, None, :] == block_owner[:, :, None]
    slot_list = lax.optimization_barrier(jnp.sum((same_owner & earlier[None, :, :]).astype(jnp.int32), axis=2)).astype(jnp.int32)
    highest = lax.Precision.HIGHEST

    def one_block(index, update):
        group_idx = (index // NBLK).astype(jnp.int32)
        pos_idx = (index % NBLK).astype(jnp.int32)
        row_blk = block_rows[group_idx, pos_idx].astype(jnp.int32)
        col_blk = block_cols[group_idx, pos_idx].astype(jnp.int32)
        owner = block_owner[group_idx, pos_idx].astype(jnp.int32)
        slot_idx = slot_list[group_idx, pos_idx].astype(jnp.int32)
        row_start = (row_blk * BS).astype(jnp.int32)
        col_start = ((group_idx * COLB + col_blk) * BS).astype(jnp.int32)
        block_grad = lax.dynamic_slice(grad_float, (row_start, col_start), (BS, BS))
        block_adam = lax.dynamic_slice(adam_dir, (row_start, col_start), (BS, BS))
        zero_idx = jnp.zeros((), jnp.int32)
        left = lax.dynamic_slice(left_root, (group_idx, owner, slot_idx, zero_idx, zero_idx), (1, 1, 1, BS, BS)).reshape(BS, BS)
        right = lax.dynamic_slice(right_root, (group_idx, owner, slot_idx, zero_idx, zero_idx), (1, 1, 1, BS, BS)).reshape(BS, BS)
        precond = jnp.dot(jnp.dot(left, block_grad, precision=highest), right, precision=highest)
        adam_sq = jnp.sum(block_adam * block_adam)
        shampoo_sq = jnp.sum(precond * precond)
        scaled = (jnp.sqrt(adam_sq / (shampoo_sq + NORM_EPS)) * precond).astype(jnp.bfloat16)
        return lax.dynamic_update_slice(update, scaled, (row_start, col_start))
    update = jnp.zeros((ROWS, COLS), jnp.bfloat16)
    update = lax.fori_loop(0, N_GROUP * NBLK, one_block, update)
    return (update, moment)
```

```python
import functools

import jax
import jax.numpy as jnp
from jax import lax
from jax.experimental import pallas as pl
from jax.experimental.pallas import tpu as pltpu
from jax.sharding import PartitionSpec as P

BS = 1024
BETA_TWO = 0.999
ADAM_EPS = 1e-08
NORM_EPS = 1e-06

ANY = pl.BlockSpec(memory_space=pl.ANY)
SMEM = pl.BlockSpec(memory_space=pltpu.SMEM)
MIB = 1 << 20


def run_copies(copies):
    for c in copies:
        c.start()
    for c in copies:
        c.wait()


def adam_kernel(g_ref, m_ref, mo_ref, part_ref):
    @pl.when(pl.program_id(0) == 0)
    def _():
        part_ref[...] = jnp.zeros_like(part_ref)

    g = g_ref[...].astype(jnp.float32)
    moment = BETA_TWO * m_ref[...] + (1.0 - BETA_TWO) * g * g
    mo_ref[...] = moment
    adam = g / (jnp.sqrt(moment) + ADAM_EPS)
    sq = adam * adam
    for b in range(sq.shape[1] // BS):
        s = jnp.sum(sq[:, b * BS : (b + 1) * BS].reshape(-1, 8, BS), axis=0)
        part_ref[:, b * BS : (b + 1) * BS] += s


def adam(gradient, second_moment):
    rows, width = gradient.shape
    tile = 64
    moment, part = pl.pallas_call(
        adam_kernel,
        grid=(rows // tile,),
        in_specs=[pl.BlockSpec((tile, width), lambda i: (i, 0))] * 2,
        out_specs=[pl.BlockSpec((tile, width), lambda i: (i, 0)), pl.BlockSpec((8, width), lambda i: (0, 0))],
        out_shape=[
            jax.ShapeDtypeStruct((rows, width), jnp.float32),
            jax.ShapeDtypeStruct((8, width), jnp.float32),
        ],
        compiler_params=pltpu.CompilerParams(vmem_limit_bytes=32 * MIB),
        name="adam",
    )(gradient, second_moment)
    return moment, jnp.sum(part.reshape(8, width // BS, BS), axis=(0, 2))


def split_kernel(slot_ref, l_ref, r_ref, lh_ref, ll_ref, rh_ref, rl_ref):
    for src, hi_ref, lo_ref in ((l_ref, lh_ref, ll_ref), (r_ref, rh_ref, rl_ref)):
        x = src[...]
        hi = x.astype(jnp.bfloat16)
        hi_ref[...] = hi
        lo_ref[...] = (x - hi.astype(jnp.float32)).astype(jnp.bfloat16)


def split_roots(slots, left, right):
    tile = 256
    spec_in = pl.BlockSpec((1, tile, BS), lambda b, i, s: (s[b], i, 0))
    spec_out = pl.BlockSpec((1, tile, BS), lambda b, i, s: (b, i, 0))
    return pl.pallas_call(
        split_kernel,
        grid_spec=pltpu.PrefetchScalarGridSpec(
            num_scalar_prefetch=1,
            grid=(2, BS // tile),
            in_specs=[spec_in] * 2,
            out_specs=[spec_out] * 4,
        ),
        out_shape=[jax.ShapeDtypeStruct((2, BS, BS), jnp.bfloat16)] * 4,
        compiler_params=pltpu.CompilerParams(vmem_limit_bytes=32 * MIB),
        name="split_roots",
    )(slots, left, right)


def pick_kernel(row_ref, src, dst, held, in_sem, sem):
    owners, cols = row_ref.shape
    run_copies([pltpu.make_async_copy(src, held, in_sem)])
    run_copies(
        [
            pltpu.make_async_copy(held.at[row_ref[d, b], :, b], dst.at[d, b], sem.at[d * cols + b])
            for d in range(owners)
            for b in range(cols)
        ]
    )


def pick_for_owners(row_of, spread):
    owners, cols = row_of.shape
    _, quarters, _, h, w = spread.shape
    return pl.pallas_call(
        pick_kernel,
        in_specs=[SMEM, ANY],
        out_specs=ANY,
        out_shape=jax.ShapeDtypeStruct((owners, cols, quarters, h, w), jnp.bfloat16),
        scratch_shapes=[
            pltpu.VMEM(spread.shape, jnp.bfloat16),
            pltpu.SemaphoreType.DMA,
            pltpu.SemaphoreType.DMA((owners * cols,)),
        ],
        name="pick_for_owners",
    )(row_of, spread)


def unpick_kernel(owner_ref, src, dst, held, sem, out_sem):
    rows, cols = owner_ref.shape
    run_copies(
        [
            pltpu.make_async_copy(src.at[owner_ref[r, b], b], held.at[r, :, b], sem.at[r * cols + b])
            for r in range(rows)
            for b in range(cols)
        ]
    )
    run_copies([pltpu.make_async_copy(held, dst, out_sem)])


def pick_from_owners(owner_of, got):
    rows, cols = owner_of.shape
    _, _, quarters, h, w = got.shape
    shape = (rows, quarters, cols, h, w)
    return pl.pallas_call(
        unpick_kernel,
        in_specs=[SMEM, ANY],
        out_specs=ANY,
        out_shape=jax.ShapeDtypeStruct(shape, jnp.bfloat16),
        scratch_shapes=[
            pltpu.VMEM(shape, jnp.bfloat16),
            pltpu.SemaphoreType.DMA((rows * cols,)),
            pltpu.SemaphoreType.DMA,
        ],
        name="pick_from_owners",
    )(owner_of, got)


def shampoo_kernel(valid_ref, norm_ref, lh, ll, rh, rl, g_in, out, g, lhv, llv, rhv, rlv, q, u, sem, osem):
    cols = g_in.shape[1]
    quarters = g_in.shape[2]
    h, w = g_in.shape[3:]
    parts = BS // w
    tile = 256

    for b in range(cols):

        @pl.when(valid_ref[b] > 0)
        def _(b=b):
            ins = []
            for k in range(quarters):
                for p in range(parts):
                    ins.append((g_in.at[pl.ds(p * (BS // quarters // h), BS // quarters // h), b, k], g.at[k, :, :, pl.ds(p * w, w)]))
            copies = [pltpu.make_async_copy(s, d, sem.at[n]) for n, (s, d) in enumerate(ins)]
            n = len(copies)
            copies += [
                pltpu.make_async_copy(s.at[b], d, sem.at[n + i])
                for i, (s, d) in enumerate(((lh, lhv), (ll, llv), (rh, rhv), (rl, rlv)))
            ]
            run_copies(copies)
            gv = g.reshape(BS, BS)

            def step(t, acc):
                rows = pl.ds(pl.multiple_of(t * tile, tile), tile)
                dot = functools.partial(jnp.dot, preferred_element_type=jnp.float32)
                p = dot(lhv[rows, :], gv[...]) + dot(llv[rows, :], gv[...])
                ph = p.astype(jnp.bfloat16)
                pl_ = (p - ph.astype(jnp.float32)).astype(jnp.bfloat16)
                qt = dot(ph, rhv[...]) + (dot(ph, rlv[...]) + dot(pl_, rhv[...]))
                q[rows, :] = qt
                return acc + jnp.sum((qt * qt).reshape(-1, 8, BS), axis=0)

            acc = lax.fori_loop(0, BS // tile, step, jnp.zeros((8, BS), jnp.float32))
            ratio = jnp.sqrt(norm_ref[b] / (jnp.sum(acc) + NORM_EPS))
            uv = u.reshape(BS, BS)

            def scale(t, c):
                rows = pl.ds(pl.multiple_of(t * 128, 128), 128)
                uv[rows, :] = (ratio * q[rows, :]).astype(jnp.bfloat16)
                return c

            lax.fori_loop(0, BS // 128, scale, 0)
            outs = []
            for k in range(quarters):
                for p in range(parts):
                    outs.append((u.at[k, :, :, pl.ds(p * w, w)], out.at[pl.ds(p * (BS // quarters // h), BS // quarters // h), b, k]))
            run_copies([pltpu.make_async_copy(s, d, osem.at[n]) for n, (s, d) in enumerate(outs)])


def shampoo(valid, norms, roots, got):
    big = (BS, BS)
    count = got.shape[2] * (BS // got.shape[4])
    four = (got.shape[2], BS // got.shape[2] // got.shape[3], got.shape[3], BS)
    return pl.pallas_call(
        shampoo_kernel,
        in_specs=[SMEM, SMEM] + [ANY] * 5,
        out_specs=ANY,
        out_shape=jax.ShapeDtypeStruct(got.shape, jnp.bfloat16),
        scratch_shapes=[pltpu.VMEM(four, jnp.bfloat16)]
        + [pltpu.VMEM(big, jnp.bfloat16)] * 4
        + [
            pltpu.VMEM(big, jnp.float32),
            pltpu.VMEM(four, jnp.bfloat16),
            pltpu.SemaphoreType.DMA((count + 4,)),
            pltpu.SemaphoreType.DMA((count,)),
        ],
        compiler_params=pltpu.CompilerParams(vmem_limit_bytes=48 * MIB),
        cost_estimate=pl.CostEstimate(flops=20 * BS**3, bytes_accessed=24 * MIB, transcendentals=0),
        name="shampoo",
    )(valid, norms, *roots, got)


def rows_kernel(place_ref, own, before, after, far_lo, far_hi, out, held, sem, out_sem):
    parts, cols, h, w = own.shape
    halves = BS // w
    depth = parts // halves
    copies = []
    n = 0
    for k, src in enumerate((own, before, after)):
        for b in range(cols):
            for p in range(halves):
                start = pl.multiple_of(place_ref[k] * (cols * BS) + (b * BS + p * w), w)
                copies.append(
                    pltpu.make_async_copy(src.at[pl.ds(p * depth, depth), b], held.at[:, :, pl.ds(start, w)], sem.at[n])
                )
                n += 1
    for p, src in enumerate((far_lo, far_hi)):
        for b in range(cols):
            start = pl.multiple_of(place_ref[3] * (cols * BS) + (b * BS + p * w), w)
            copies.append(pltpu.make_async_copy(src.at[:, b], held.at[:, :, pl.ds(start, w)], sem.at[n]))
            n += 1
    run_copies(copies)
    run_copies([pltpu.make_async_copy(held, out, out_sem)])


def gather_groups(pieces):
    parts, cols, h, w = pieces.shape
    halves = BS // w
    depth = parts // halves
    groups = lax.axis_size("group")
    me = lax.axis_index("group")
    up = [(i, (i + 1) % groups) for i in range(groups)]
    down = [(i, (i - 1) % groups) for i in range(groups)]
    before = lax.ppermute(pieces, "group", up)
    after = lax.ppermute(pieces, "group", down)
    far_lo = lax.ppermute(before[:depth], "group", up)
    far_hi = lax.ppermute(after[depth:], "group", down)
    place = jnp.stack([me, (me + groups - 1) % groups, (me + 1) % groups, (me + 2) % groups]).astype(jnp.int32)
    rows = pl.pallas_call(
        rows_kernel,
        in_specs=[SMEM] + [ANY] * 5,
        out_specs=ANY,
        out_shape=jax.ShapeDtypeStruct((depth, h, groups * cols * BS), jnp.bfloat16),
        scratch_shapes=[
            pltpu.VMEM((depth, h, groups * cols * BS), jnp.bfloat16),
            pltpu.SemaphoreType.DMA((4 * cols * halves,)),
            pltpu.SemaphoreType.DMA,
        ],
        compiler_params=pltpu.CompilerParams(vmem_limit_bytes=16 * MIB),
        name="whole_rows",
    )(place, pieces, before, after, far_lo, far_hi)
    return rows.reshape(depth * h, groups * cols * BS)


def gather_partials(partial):
    cols = partial.shape[0]
    wide = jnp.broadcast_to(jnp.pad(partial, (0, 128 - cols))[None, :], (8, 128))
    return lax.all_gather(wide, "fsdp", axis=0)[:, 0, :cols]


def on_device(gradient, second_moment, left_root, right_root, block_rows, block_cols, block_owner):
    shard_rows, width = gradient.shape
    cols = width // BS
    fsdp = lax.axis_size("fsdp")
    me = lax.axis_index("fsdp")
    group = lax.axis_index("group")
    quarters = BS // shard_rows
    row_count = fsdp // quarters
    h = 16
    halves = fsdp * h // shard_rows
    w = BS // halves
    pick = lambda t: lax.dynamic_index_in_dim(t, group, 0, keepdims=False)
    rows_list, cols_list, owner_list = pick(block_rows), pick(block_cols), pick(block_owner)

    count = rows_list.shape[0]
    pos = jnp.arange(count, dtype=jnp.int32)
    slot_list = jnp.sum((owner_list[None, :] == owner_list[:, None]) & (pos[None, :] < pos[:, None]), axis=1, dtype=jnp.int32)
    col_is = cols_list[None, :] == jnp.arange(cols, dtype=jnp.int32)[:, None]
    at_owner = (owner_list[None, None, :] == jnp.arange(fsdp, dtype=jnp.int32)[:, None, None]) & col_is[None]
    row_of = jnp.sum(jnp.where(at_owner, rows_list, 0), axis=2, dtype=jnp.int32)
    at_row = (rows_list[None, None, :] == jnp.arange(row_count, dtype=jnp.int32)[:, None, None]) & col_is[None]
    owner_of = jnp.sum(jnp.where(at_row, owner_list, 0), axis=2, dtype=jnp.int32)
    mine = (owner_list[None, :] == me) & col_is
    my_slot = jnp.sum(jnp.where(mine, slot_list, 0), axis=1, dtype=jnp.int32)
    my_row = jnp.sum(jnp.where(mine, rows_list, 0), axis=1, dtype=jnp.int32)
    my_valid = jnp.sum(mine, axis=1, dtype=jnp.int32)

    mixed = gradient.reshape(shard_rows // h, h, cols, halves, w).transpose(3, 0, 2, 1, 4)
    spread = lax.all_to_all(mixed.reshape(fsdp, cols, h, w), "fsdp", 0, 0, tiled=True)
    moment, partial = adam(gradient, second_moment)
    row_norm = jnp.sum(gather_partials(partial).reshape(row_count, quarters, cols), axis=1)
    norms = jnp.sum(
        jnp.where(my_row[None, :] == jnp.arange(row_count, dtype=jnp.int32)[:, None], row_norm, 0.0), axis=0
    )
    roots = split_roots(my_slot, left_root[0, 0], right_root[0, 0])

    send = pick_for_owners(row_of, spread.reshape(row_count, quarters, cols, h, w))
    got = lax.all_to_all(send, "fsdp", 0, 0, tiled=True)
    reply = shampoo(my_valid, norms, roots, got)
    back = lax.all_to_all(reply, "fsdp", 0, 0, tiled=True)
    home = pick_from_owners(owner_of, back)
    pieces = lax.all_to_all(home.reshape(fsdp, cols, h, w), "fsdp", 0, 0, tiled=True)
    return gather_groups(pieces), moment


def solution(mesh):
    placed = (
        P("fsdp", "group"),
        P("fsdp", "group"),
        P("group", "fsdp", None, None, None),
        P("group", "fsdp", None, None, None),
        P(),
        P(),
        P(),
    )
    return jax.shard_map(
        on_device,
        mesh=mesh,
        in_specs=placed,
        out_specs=(P("fsdp", None), P("fsdp", "group")),
        check_vma=False,
    )
```

```python
import functools

import jax
import jax.numpy as jnp
from jax import lax
from jax.experimental import pallas as pl
from jax.experimental.pallas import tpu as pltpu
from jax.sharding import PartitionSpec as P

BS = 1024
BETA_TWO = 0.999
ADAM_EPS = 1e-08
NORM_EPS = 1e-06

ANY = pl.BlockSpec(memory_space=pl.ANY)
SMEM = pl.BlockSpec(memory_space=pltpu.SMEM)
MIB = 1 << 20


def run_copies(copies):
    for c in copies:
        c.start()
    for c in copies:
        c.wait()


def adam_kernel(g_ref, m_ref, mo_ref, norm_ref, acc):
    step, cols = pl.program_id(0), acc.shape[1] // BS

    @pl.when(step == 0)
    def _():
        acc[...] = jnp.zeros_like(acc)

    g = g_ref[...].astype(jnp.float32)
    moment = BETA_TWO * m_ref[...] + (1.0 - BETA_TWO) * g * g
    mo_ref[...] = moment
    adam = g / (jnp.sqrt(moment) + ADAM_EPS)
    acc[...] += jnp.sum((adam * adam).reshape(-1, 8, acc.shape[1]), axis=0)

    @pl.when(step == pl.num_programs(0) - 1)
    def _():
        row = lax.broadcasted_iota(jnp.int32, norm_ref.shape, 0)
        lane = lax.broadcasted_iota(jnp.int32, norm_ref.shape, 1)
        rest = jnp.zeros(norm_ref.shape, jnp.float32)
        for b in range(cols):
            rest = jnp.where(lane == b, jnp.sum(acc[:, b * BS : (b + 1) * BS]), rest)
        out = jnp.zeros(norm_ref.shape, jnp.float32)
        for term in range(3):
            now = rest.astype(jnp.bfloat16).astype(jnp.float32)
            out = jnp.where(row == term, now, out)
            rest = rest - now
        norm_ref[...] = out.astype(jnp.bfloat16)


def adam(gradient, second_moment):
    rows, width = gradient.shape
    tile = 64
    return pl.pallas_call(
        adam_kernel,
        grid=(rows // tile,),
        in_specs=[pl.BlockSpec((tile, width), lambda i: (i, 0))] * 2,
        out_specs=[pl.BlockSpec((tile, width), lambda i: (i, 0)), pl.BlockSpec((16, 128), lambda i: (0, 0))],
        out_shape=[
            jax.ShapeDtypeStruct((rows, width), jnp.float32),
            jax.ShapeDtypeStruct((16, 128), jnp.bfloat16),
        ],
        scratch_shapes=[pltpu.VMEM((8, width), jnp.float32)],
        compiler_params=pltpu.CompilerParams(vmem_limit_bytes=56 * MIB),
        name="adam",
    )(gradient, second_moment)


RING = 4


def tables_kernel(rows_ref, cols_ref, owner_ref, place_ref, spread, fwd0, fwd1, back0, back1, from0, from1, offs, mine, far, row_of, owner_of):
    count = rows_ref.shape[1]
    devices, cols = row_of.shape
    me, group = place_ref[0], place_ref[1]
    for b in range(cols):
        for r in range(owner_of.shape[0]):
            owner_of[r, b] = 0
        for d in range(devices):
            row_of[d, b] = 0
        mine[0, b] = 0
        mine[1, b] = 0
        mine[2, b] = 0
    seen = jnp.int32(0)
    for k in range(count):
        r, b, o = rows_ref[group, k], cols_ref[group, k], owner_ref[group, k]
        row_of[o, b] = r
        owner_of[r, b] = o

        @pl.when(o == me)
        def _(r=r, b=b, seen=seen):
            mine[0, b] = seen
            mine[1, b] = 1
            mine[2, b] = r

        seen = seen + (o == me).astype(jnp.int32)

    c = me % 2
    y = (me // 2) % RING
    x = me // (2 * RING)
    yh, yl = y // 2, y % 2
    upper = c == 0
    sel = lambda a, b: jnp.where(upper, a, b)
    p_first, p_second = sel(x, y), sel(y, x)
    wrap = lambda v: (v + 2 * RING) % RING
    spread[0] = c
    sent = []
    for k, place in enumerate((2 * yh, 2 - 2 * yh, 2 * yh + 1, 3 - 2 * yh)):
        sent.append(sel(place, wrap(x + k)))
        spread[1 + k] = sent[k]
        spread[5 + k] = sel(place, wrap(x - k))
    for b, fwd in enumerate((fwd0, fwd1)):
        for flip in range(2):
            for k in range(RING):
                to = wrap(p_second + k)
                core = jnp.where(upper, flip, 1 - flip)
                row = row_of[sel((x * RING + to) * 2 + core, (to * RING + y) * 2 + core), b]
                for t in range(2):
                    n = (flip * RING + k) * 2 + t
                    inner = 2 * (row % 2) + t
                    fwd[0, n] = wrap(p_first - sel(row // 2, inner))
                    fwd[1, n] = sel(inner, row // 2)
    for b, (back, frm) in enumerate(((back0, from0), (back1, from1))):
        for k in range(RING):
            to = wrap(p_first + k)
            for u in range(4):
                owner = owner_of[sel(to * 2 + u // 2, u * 2 + to // 2), b]
                ox, oy, oc = owner // (2 * RING), (owner // 2) % RING, owner % 2
                back[0, k * 4 + u] = jnp.where(oc == c, 0, RING) + wrap(sel(oy, ox) - p_second)
                back[1, k * 4 + u] = sel(u % 2, to % 2)
        for k in range(4):
            owner = owner_of[sel(2 * x + sent[k] // 2, sent[k] * 2 + yh), b]
            ox, oy = owner // (2 * RING), (owner // 2) % RING
            frm[0, k] = wrap(p_first - sel(ox, oy))
            frm[1, k] = sent[k]
    for flip in range(2):
        from_upper = c == flip
        for k in range(RING):
            y_from, x_from = wrap(y - k), wrap(x - k)
            for t in range(2):
                for e in range(2):
                    up = ((y_from % 2) * 2 + e) * 256 + (y_from // 2) * 64 + t * 32
                    low = (t * 2 + e) * 256 + 128 + x_from * 32
                    offs[((flip * RING + k) * 2 + t) * 2 + e] = jnp.where(from_upper, up, low)
    for i, step in enumerate((0, 0, 3, 3, 1, 1, 2, 2)):
        far[0, i] = (group + step) % 4
        far[1, i] = c if i % 2 == 0 else 1 - c


def make_tables(rows, cols, owner, place, devices, col_count, row_count):
    i32 = lambda *shape: jax.ShapeDtypeStruct(shape, jnp.int32)
    shapes = [i32(9)] + [i32(2, 16)] * 4 + [i32(2, 4)] * 2 + [i32(32), i32(3, col_count), i32(2, 8)]
    shapes += [i32(devices, col_count), i32(row_count, col_count)]
    return pl.pallas_call(
        tables_kernel,
        in_specs=[SMEM] * 4,
        out_specs=[SMEM] * len(shapes),
        out_shape=shapes,
        name="tables",
    )(rows, cols, owner, place)


def stage_all(bufs, held, sems):
    copies = [pltpu.make_async_copy(src, held.at[i], sems.at[i]) for i, src in enumerate(bufs)]
    run_copies(copies)


def table_mover(name, table, ins, outs, pieces, piece_shape):
    n_in, n_out = len(ins), len(outs)

    def kernel(tab, *refs):
        srcs, dsts = refs[:n_in], refs[n_in : n_in + n_out]
        held, in_sem, out_sem = refs[n_in + n_out :]
        plan = pieces(tab, srcs, dsts)
        for i, (choices, _) in enumerate(plan):
            for cond, src in choices:
                copy = pltpu.make_async_copy(src, held.at[i], in_sem.at[i])
                if cond is None:
                    copy.start()
                else:
                    pl.when(cond)(copy.start)
        for i, (choices, dst) in enumerate(plan):
            pltpu.make_async_copy(choices[0][1], held.at[i], in_sem.at[i]).wait()
            pltpu.make_async_copy(held.at[i], dst, out_sem.at[i]).start()
        for i, (_, dst) in enumerate(plan):
            pltpu.make_async_copy(held.at[i], dst, out_sem.at[i]).wait()

    count = pieces.count
    size = 2 * count
    for d in piece_shape:
        size *= d
    return pl.pallas_call(
        kernel,
        in_specs=[SMEM] + [ANY] * n_in,
        out_specs=[ANY] * n_out,
        out_shape=[jax.ShapeDtypeStruct(o, jnp.bfloat16) for o in outs],
        scratch_shapes=[
            pltpu.VMEM((count, *piece_shape), jnp.bfloat16),
            pltpu.SemaphoreType.DMA((count,)),
            pltpu.SemaphoreType.DMA((count,)),
        ],
        compiler_params=pltpu.CompilerParams(vmem_limit_bytes=16 * MIB),
        cost_estimate=pl.CostEstimate(flops=0, bytes_accessed=2 * size, transcendentals=0),
        name=name,
    )(table, *ins)


def counted(count):
    def mark(f):
        f.count = count
        return f

    return mark


def picker(name, table, bufs, out_groups, outs_per, piece_shape, src_b=None, dst_b=None, before=()):
    n_in = len(bufs)
    per_buf = bufs[0].shape[0 if src_b is None else 1]

    def kernel(tab, *refs):
        srcs, dsts = refs[:n_in], refs[n_in + len(before) :][:out_groups]
        held, in_sem, out_sem = refs[n_in + len(before) + out_groups :]
        run_copies(
            [
                pltpu.make_async_copy(src if src_b is None else src.at[src_b], held.at[i], in_sem.at[i])
                for i, src in enumerate(srcs)
            ]
        )
        run_copies(
            [
                pltpu.make_async_copy(
                    held.at[tab[0, i * outs_per + j], tab[1, i * outs_per + j]],
                    dsts[i].at[j] if dst_b is None else dsts[i].at[dst_b, j],
                    out_sem.at[i * outs_per + j],
                )
                for i in range(out_groups)
                for j in range(outs_per)
            ]
        )

    size = 2
    for d in piece_shape:
        size *= d
    lead = () if dst_b is None else (2,)
    return pl.pallas_call(
        kernel,
        in_specs=[SMEM] + [ANY] * (n_in + len(before)),
        out_specs=[ANY] * out_groups,
        out_shape=[jax.ShapeDtypeStruct((*lead, outs_per, *piece_shape), jnp.bfloat16)] * out_groups,
        input_output_aliases={1 + n_in + i: i for i in range(len(before))},
        scratch_shapes=[
            pltpu.VMEM((n_in, per_buf, *piece_shape), jnp.bfloat16),
            pltpu.SemaphoreType.DMA((n_in,)),
            pltpu.SemaphoreType.DMA((out_groups * outs_per,)),
        ],
        compiler_params=pltpu.CompilerParams(vmem_limit_bytes=16 * MIB),
        cost_estimate=pl.CostEstimate(
            flops=0, bytes_accessed=size * (n_in * per_buf + out_groups * outs_per), transcendentals=0
        ),
        name=name,
    )(table, *bufs, *before)


def halves(v):
    hi = v.astype(jnp.bfloat16)
    return hi, (v - hi.astype(jnp.float32)).astype(jnp.bfloat16)


def column_copies(buf, box, to_box, sem):
    h, w = 64, 128
    depth, quarters = 4, 4
    made = []
    for k in range(quarters):
        for p in range(BS // w):
            away = buf.at[pl.ds(p * depth, depth), pl.ds(k * h, h), :]
            here = box.reshape(quarters, depth, h, BS).at[k, :, :, pl.ds(p * w, w)]
            n = k * (BS // w) + p
            made.append(pltpu.make_async_copy(*((away, here) if to_box else (here, away)), sem.at[n]))
    return made


def ring_copies(bufs, box, off_ref, to_box, sem):
    made = []
    for j, buf in enumerate(bufs):
        for t in range(2):
            for e in range(2):
                n = j * 4 + t * 2 + e
                here = box.at[pl.ds(pl.multiple_of(off_ref[n], 32), 32), :]
                away = buf.at[t, e]
                made.append(pltpu.make_async_copy(*((away, here) if to_box else (here, away)), sem.at[n]))
    return made


def shampoo_kernel(b, n_bufs, mine_ref, off_ref, norm_ref, left_ref, right_ref, *refs):
    ins, outs = refs[:n_bufs], refs[n_bufs : 2 * n_bufs]
    g, lv, rv, rhv, rlv, q, u, acc, norms, g_sem, root_sem, norm_sem, out_sem = refs[2 * n_bufs :]
    tile = 256
    tiles = BS // tile
    slot = mine_ref[0, b]

    def left_load(t):
        rows = pl.ds(pl.multiple_of(t * tile, tile), tile)
        return pltpu.make_async_copy(left_ref.at[0, 0, slot, rows, :], lv.at[rows, :], root_sem.at[t])

    right_load = pltpu.make_async_copy(right_ref.at[0, 0, slot], rv, root_sem.at[tiles])

    def moves(bufs, box, to_box, sem):
        if n_bufs == 1:
            return column_copies(bufs[0], box, to_box, sem)
        return ring_copies(bufs, box, off_ref, to_box, sem)

    norm_load = pltpu.make_async_copy(norm_ref.at[:, pl.ds(256, 16), :], norms, norm_sem)
    dot = functools.partial(jnp.dot, preferred_element_type=jnp.float32)

    @pl.when(mine_ref[1, b] > 0)
    def _():
        grads = moves(ins, g, True, g_sem)
        left_load(0).start()
        for c in grads:
            c.start()
        for t in range(1, tiles):
            left_load(t).start()
        right_load.start()
        norm_load.start()
        for c in grads:
            c.wait()
        acc[...] = jnp.zeros_like(acc)

        def step(t, carry):
            rows = pl.ds(pl.multiple_of(t * tile, tile), tile)
            left_load(t).wait()
            lh, ll = halves(lv[rows, :])
            ph, plow = halves(dot(lh, g[...]) + dot(ll, g[...]))

            @pl.when(t == 0)
            def _():
                right_load.wait()

                def split(i, carry):
                    part = pl.ds(pl.multiple_of(i * 128, 128), 128)
                    rhv[part, :], rlv[part, :] = halves(rv[part, :])
                    return carry

                lax.fori_loop(0, BS // 128, split, 0)

            qt = dot(ph, rhv[...]) + (dot(ph, rlv[...]) + dot(plow, rhv[...]))
            q[rows, :] = qt
            acc[...] += jnp.sum((qt * qt).reshape(-1, 8, BS), axis=0)
            return carry

        lax.fori_loop(0, tiles, step, 0)
        norm_load.wait()
        device = lax.broadcasted_iota(jnp.int32, norms.shape, 0)
        lane = lax.broadcasted_iota(jnp.int32, norms.shape, 2)
        wanted = (device // 4 == mine_ref[2, b]) & (lane == b)
        adam_sq = jnp.sum(jnp.where(wanted, norms[...].astype(jnp.float32), 0.0))
        ratio = jnp.sqrt(adam_sq / (jnp.sum(acc[...]) + NORM_EPS))

        def scale(t, carry):
            rows = pl.ds(pl.multiple_of(t * 128, 128), 128)
            u[rows, :] = (ratio * q[rows, :]).astype(jnp.bfloat16)
            return carry

        lax.fori_loop(0, BS // 128, scale, 0)
        run_copies(moves(outs, u, False, out_sem))


def shampoo(b, mine, offsets, norms, left_root, right_root, bufs, out):
    big = (BS, BS)
    return pl.pallas_call(
        functools.partial(shampoo_kernel, b, len(bufs)),
        in_specs=[SMEM] * 2 + [ANY] * (3 + len(bufs)),
        out_specs=[ANY] * len(bufs),
        out_shape=[jax.ShapeDtypeStruct(out, jnp.bfloat16)] * len(bufs),
        scratch_shapes=[
            pltpu.VMEM(big, jnp.bfloat16),
            pltpu.VMEM(big, jnp.float32),
            pltpu.VMEM(big, jnp.float32),
            pltpu.VMEM(big, jnp.bfloat16),
            pltpu.VMEM(big, jnp.bfloat16),
            pltpu.VMEM(big, jnp.float32),
            pltpu.VMEM(big, jnp.bfloat16),
            pltpu.VMEM((8, BS), jnp.float32),
            pltpu.VMEM((norms.shape[0], 16, 128), jnp.bfloat16),
            pltpu.SemaphoreType.DMA((32,)),
            pltpu.SemaphoreType.DMA((8,)),
            pltpu.SemaphoreType.DMA,
            pltpu.SemaphoreType.DMA((32,)),
        ],
        compiler_params=pltpu.CompilerParams(vmem_limit_bytes=58 * MIB),
        cost_estimate=pl.CostEstimate(flops=10 * BS**3, bytes_accessed=12 * MIB, transcendentals=0),
        name="shampoo",
    )(mine, offsets, norms, left_root, right_root, *bufs)


def pick_kernel(b, row_ref, src, norm, dst, held, sent, in_sem, norm_sem, sem):
    owners, (_, h, _) = row_ref.shape[0], src.shape
    run_copies([pltpu.make_async_copy(src, held, in_sem), pltpu.make_async_copy(norm, sent, norm_sem)])
    run_copies(
        [
            pltpu.make_async_copy(held.at[row_ref[d, b]], dst.at[d, pl.ds(0, h), :], sem.at[0, d])
            for d in range(owners)
        ]
        + [pltpu.make_async_copy(sent, dst.at[d, pl.ds(h, sent.shape[0]), :], sem.at[1, d]) for d in range(owners)]
    )


def pick_for_owners(b, row_of, spread, norm):
    owners = row_of.shape[0]
    _, h, w = spread.shape
    return pl.pallas_call(
        functools.partial(pick_kernel, b),
        in_specs=[SMEM, ANY, ANY],
        out_specs=ANY,
        out_shape=jax.ShapeDtypeStruct((owners, h + norm.shape[0], w), jnp.bfloat16),
        scratch_shapes=[
            pltpu.VMEM(spread.shape, jnp.bfloat16),
            pltpu.VMEM(norm.shape, jnp.bfloat16),
            pltpu.SemaphoreType.DMA,
            pltpu.SemaphoreType.DMA,
            pltpu.SemaphoreType.DMA((2, owners)),
        ],
        compiler_params=pltpu.CompilerParams(vmem_limit_bytes=16 * MIB),
        cost_estimate=pl.CostEstimate(flops=0, bytes_accessed=3 * MIB, transcendentals=0),
        name="pick_for_owners",
    )(row_of, spread, norm)


def unpick_kernel(b, owner_ref, src, dst, held, sem, out_sem):
    rows = owner_ref.shape[0]
    run_copies([pltpu.make_async_copy(src.at[owner_ref[r, b]], held.at[r], sem.at[r]) for r in range(rows)])
    run_copies([pltpu.make_async_copy(held, dst, out_sem)])


def pick_from_owners(b, owner_of, got):
    shape = (owner_of.shape[0], *got.shape[1:])
    return pl.pallas_call(
        functools.partial(unpick_kernel, b),
        in_specs=[SMEM, ANY],
        out_specs=ANY,
        out_shape=jax.ShapeDtypeStruct(shape, jnp.bfloat16),
        scratch_shapes=[
            pltpu.VMEM(shape, jnp.bfloat16),
            pltpu.SemaphoreType.DMA((shape[0],)),
            pltpu.SemaphoreType.DMA,
        ],
        compiler_params=pltpu.CompilerParams(vmem_limit_bytes=16 * MIB),
        cost_estimate=pl.CostEstimate(flops=0, bytes_accessed=1 * MIB, transcendentals=0),
        name="pick_from_owners",
    )(owner_of, got)


def column_rows_kernel(b, cols, tab, own, before, after, far_lo, far_hi, out, held, sem, out_sem):
    parts, h, w = own.shape
    sides = BS // w
    depth = parts // sides
    copies = []
    for k, src in enumerate((own, before, after)):
        for p in range(sides):
            copies.append((src.at[pl.ds(p * depth, depth)], held.at[k, :, :, pl.ds(p * w, w)]))
    for half, src in enumerate((far_lo, far_hi)):
        for p in range(sides // 2):
            lanes = pl.ds((half * (sides // 2) + p) * w, w)
            copies.append((src.at[pl.ds(p * depth, depth)], held.at[3, :, :, lanes]))
    run_copies([pltpu.make_async_copy(s, d, sem.at[n]) for n, (s, d) in enumerate(copies)])
    puts = []
    for k, i in enumerate((0, 2, 4, 6)):
        col = pl.multiple_of(tab[0, i] * (cols * BS) + b * BS, BS)
        puts.append(
            pltpu.make_async_copy(held.at[k].reshape(depth * h, BS), out.at[:, pl.ds(col, BS)], out_sem.at[k])
        )
    run_copies(puts)


def column_rows(b, cols, groups, table, bufs):
    parts, h, w = bufs[0].shape
    depth = parts * w // BS
    return pl.pallas_call(
        functools.partial(column_rows_kernel, b, cols),
        in_specs=[SMEM] + [ANY] * 5,
        out_specs=ANY,
        out_shape=jax.ShapeDtypeStruct((depth * h, groups * cols * BS), jnp.bfloat16),
        scratch_shapes=[
            pltpu.VMEM((4, depth, h, BS), jnp.bfloat16),
            pltpu.SemaphoreType.DMA((4 * BS // w,)),
            pltpu.SemaphoreType.DMA((4,)),
        ],
        compiler_params=pltpu.CompilerParams(vmem_limit_bytes=16 * MIB),
        cost_estimate=pl.CostEstimate(flops=0, bytes_accessed=4 * MIB, transcendentals=0),
        name="column_rows",
    )(table, *bufs)


def rows_kernel(b, cols, tab, *refs):
    ins, out = refs[:8], refs[-4]
    held, in_sem, out_sem = refs[-3:]
    h = ins[0].shape[0]
    copies = [pltpu.make_async_copy(src, held.at[i], in_sem.at[i]) for i, src in enumerate(ins)]
    for c in copies:
        c.start()
    puts = []
    for i in range(8):
        row = pl.multiple_of(tab[1, i] * h, h)
        col = pl.multiple_of(tab[0, i] * (cols * BS) + b * BS, BS)
        copies[i].wait()
        put = pltpu.make_async_copy(held.at[i], out.at[pl.ds(row, h), pl.ds(col, BS)], out_sem.at[i])
        put.start()
        puts.append(put)
    for put in puts:
        put.wait()


def whole_rows(b, cols, groups, table, bufs, before):
    h = bufs[0].shape[0]
    shape = jax.ShapeDtypeStruct((2 * h, groups * cols * BS), jnp.bfloat16)
    extra = [] if before is None else [before]
    return pl.pallas_call(
        functools.partial(rows_kernel, b, cols),
        in_specs=[SMEM] + [ANY] * (8 + len(extra)),
        out_specs=ANY,
        out_shape=shape,
        input_output_aliases={9: 0} if extra else {},
        scratch_shapes=[
            pltpu.VMEM((8, h, BS), jnp.bfloat16),
            pltpu.SemaphoreType.DMA((8,)),
            pltpu.SemaphoreType.DMA((8,)),
        ],
        compiler_params=pltpu.CompilerParams(vmem_limit_bytes=16 * MIB),
        cost_estimate=pl.CostEstimate(flops=0, bytes_accessed=4 * MIB, transcendentals=0),
        name="whole_rows",
    )(table, *bufs, *extra)


def permute(value, move):
    pairs = []
    for x in range(RING):
        for y in range(RING):
            for c in range(2):
                to = move(x, y, c)
                if to is not None:
                    tx, ty, tc = to
                    pairs.append(((x * RING + y) * 2 + c, ((tx % RING) * RING + ty % RING) * 2 + tc))
    return lax.ppermute(value, "fsdp", pairs)


def swap_cores(value):
    return permute(value, lambda x, y, c: (x, y, 1 - c))


def along_first(value, k):
    return permute(value, lambda x, y, c: (x + k, y, c) if c == 0 else (x, y + k, c))


def along_second(value, k, flip):
    return permute(value, lambda x, y, c: (x, y + k, c ^ flip) if c == 0 else (x + k, y, c ^ flip))


def back_second(value, k, flip):
    return permute(value, lambda x, y, c: (x, y - k, c ^ flip) if c ^ flip == 0 else (x - k, y, c ^ flip))


def spread_move(value, k):
    return permute(value, lambda x, y, c: (x + k, y, c) if c == 1 else ((x, y + 2, c) if k != 2 else None))


def on_device(gradient, second_moment, left_root, right_root, block_rows, block_cols, block_owner):
    shard_rows, width = gradient.shape
    cols = width // BS
    fsdp = lax.axis_size("fsdp")
    groups = lax.axis_size("group")
    me = lax.axis_index("fsdp")
    group = lax.axis_index("group")
    quarters = BS // shard_rows
    row_count = fsdp // quarters
    half = shard_rows // 2
    part = half // 4
    place = jnp.stack([me, group]).astype(jnp.int32)
    up = [(i, (i + 1) % groups) for i in range(groups)]
    down = [(i, (i - 1) % groups) for i in range(groups)]
    across = lambda v, w: lax.ppermute(v, "group", w)
    every = lambda v: lax.all_to_all(v, "fsdp", 0, 0, tiled=True)

    h, w = 64, 128
    mixed = gradient[:, :BS].reshape(shard_rows // h, h, BS // w, w).transpose(2, 0, 1, 3)
    spread = every(mixed.reshape(fsdp, h, w))

    give = lax.dynamic_slice(gradient, ((1 - me % 2) * half, BS), (half, BS))
    other = swap_cores(give)
    moment, norm = adam(gradient, second_moment)
    tables = make_tables(block_rows, block_cols, block_owner, place, fsdp, cols, row_count)
    spread_tab, _, fwd, _, back_tab, _, from_tab, offsets, mine, far_tab, row_of, owner_of = tables

    lanes = pl.ds(BS, BS)

    @counted(6)
    def spread_pieces(tab, ins, outs):
        mine_ref, other_ref = ins
        core = tab[0]
        made = []
        for k in (1, 2, 3):
            at = pl.multiple_of(tab[1 + k] * part, part)
            here = pl.multiple_of(core * half + at, part)
            made.append(([(None, mine_ref.at[pl.ds(here, part), lanes])], outs[k - 1].at[core]))
            made.append(([(None, other_ref.at[pl.ds(at, part), :])], outs[k - 1].at[1 - core]))
        return made

    sends = table_mover("spread_send", spread_tab, [gradient, other], [(2, part, BS)] * 3, spread_pieces, (part, BS))
    arrived = {k: spread_move(sends[k - 1], k) for k in (1, 3, 2)}
    arrived = [arrived[k] for k in (1, 2, 3)]

    @counted(8)
    def stack_pieces(tab, ins, outs):
        mine_ref, other_ref, got = ins[0], ins[1], ins[2:]
        core = tab[0]
        made = []
        for k in range(4):
            u = tab[5 + k]
            at = pl.multiple_of(tab[5 + k] * part, part)
            here = pl.multiple_of(core * half + at, part)
            local = (mine_ref.at[pl.ds(here, part), lanes], other_ref.at[pl.ds(at, part), :])
            for e in range(2):
                src_e = core if e == 0 else 1 - core
                if k == 0:
                    choices = [(None, local[e])]
                elif k == 2:
                    choices = [(core == 0, local[e]), (core == 1, got[1].at[src_e])]
                else:
                    choices = [(None, got[k - 1].at[src_e])]
                made.append((choices, outs[0].at[u, src_e]))
        return made

    (stacked,) = table_mover(
        "spread_stack", spread_tab, [gradient, other, *arrived], [(4, 2, part, BS)], stack_pieces, (part, BS)
    )
    stacked, spread = lax.optimization_barrier((stacked, spread))

    picked0 = pick_for_owners(0, row_of, spread.reshape(row_count, quarters * h, w), norm)
    got = {k: along_first(stacked, k) for k in (1, 3, 2)}
    picked0, got = lax.optimization_barrier((picked0, got))
    got0 = every(picked0)
    picked = picker("to_owners", fwd, [stacked, got[1], got[2], got[3]], 8, 2, (2, part, BS))
    far_pieces = [(0, 1), (0, 3), (1, 1), (1, 3), (0, 2), (1, 2), (1, 0)]
    bufs = {(0, 0): picked[0]}
    for f, k in far_pieces:
        bufs[f, k] = along_second(picked[f * 4 + k], k, f)

    got0, bufs = lax.optimization_barrier((got0, bufs))
    (done0,) = shampoo(0, mine, offsets, got0, left_root, right_root, [got0], (fsdp, quarters * h, w))
    bufs = [bufs[f, k] for f in range(2) for k in range(4)]
    done = shampoo(1, mine, offsets, got0, left_root, right_root, bufs, bufs[0].shape)

    home0 = every(pick_from_owners(0, owner_of, every(done0)).reshape(fsdp, h, w))
    before, after = across(home0, up), across(home0, down)
    far_lo, far_hi = across(before[: fsdp // 2], up), across(after[fsdp // 2 :], down)
    update = column_rows(0, cols, groups, far_tab, [home0, before, after, far_lo, far_hi])

    back = {(0, 0): done[0]}
    for f, k in far_pieces:
        back[f, k] = back_second(done[f * 4 + k], k, f)
    back = [back[f, k] for f in range(2) for k in range(4)]
    replies = picker("to_homes", back_tab, back, 4, 4, (2, part, BS))
    held = {k: along_first(replies[k], k) for k in (1, 3, 2)}
    held = [replies[0]] + [held[k] for k in (1, 2, 3)]
    slots = picker("from_owners", from_tab, held, 4, 1, (2, part, BS))
    arrived = [spread_move(slots[k][0], k) for k in (1, 2, 3)]

    @counted(8)
    def home_pieces(tab, ins, outs):
        core = tab[0]
        made = []
        for k in range(4):
            at = pl.multiple_of(tab[5 + k] * part, part)
            for i, e in enumerate((core, 1 - core)):
                if k == 2:
                    choices = [(core == 0, ins[1].at[0, e]), (core == 1, ins[3].at[e])]
                elif k == 0:
                    choices = [(None, ins[0].at[0, e])]
                else:
                    choices = [(None, ins[1 + k].at[e])]
                made.append((choices, outs[i].at[pl.ds(at, part), :]))
        return made

    keep, give = table_mover(
        "home", spread_tab, [slots[0], slots[2], *arrived], [(half, BS)] * 2, home_pieces, (part, BS)
    )
    got = swap_cores(give)
    k_up, k_down, g_up, g_down = across(keep, up), across(keep, down), across(got, up), across(got, down)
    k_far, g_far = across(k_up, up), across(g_down, down)
    update = whole_rows(
        1, cols, groups, far_tab, [keep, got, k_up, g_up, k_down, g_down, k_far, g_far], update
    )
    return update, moment


def solution(mesh):
    placed = (
        P("fsdp", "group"),
        P("fsdp", "group"),
        P("group", "fsdp", None, None, None),
        P("group", "fsdp", None, None, None),
        P(),
        P(),
        P(),
    )
    return jax.shard_map(
        on_device,
        mesh=mesh,
        in_specs=placed,
        out_specs=(P("fsdp", None), P("fsdp", "group")),
        check_vma=False,
    )
```

```python
import functools

import jax
import jax.numpy as jnp
from jax import lax
from jax.experimental import pallas as pl
from jax.experimental.pallas import tpu as pltpu
from jax.sharding import PartitionSpec as P

BS = 1024
BETA_TWO = 0.999
ADAM_EPS = 1e-08
NORM_EPS = 1e-06

ANY = pl.BlockSpec(memory_space=pl.ANY)
SMEM = pl.BlockSpec(memory_space=pltpu.SMEM)
MIB = 1 << 20


def run_copies(copies):
    for c in copies:
        c.start()
    for c in copies:
        c.wait()


def adam_kernel(g_ref, m_ref, mo_ref, norm_ref, acc):
    step, cols = pl.program_id(0), acc.shape[1] // BS

    @pl.when(step == 0)
    def _():
        acc[...] = jnp.zeros_like(acc)

    g = g_ref[...].astype(jnp.float32)
    moment = BETA_TWO * m_ref[...] + (1.0 - BETA_TWO) * g * g
    mo_ref[...] = moment
    adam = g / (jnp.sqrt(moment) + ADAM_EPS)
    acc[...] += jnp.sum((adam * adam).reshape(-1, 8, acc.shape[1]), axis=0)

    @pl.when(step == pl.num_programs(0) - 1)
    def _():
        row = lax.broadcasted_iota(jnp.int32, norm_ref.shape, 0)
        lane = lax.broadcasted_iota(jnp.int32, norm_ref.shape, 1)
        rest = jnp.zeros(norm_ref.shape, jnp.float32)
        for b in range(cols):
            rest = jnp.where(lane == b, jnp.sum(acc[:, b * BS : (b + 1) * BS]), rest)
        out = jnp.zeros(norm_ref.shape, jnp.float32)
        for term in range(3):
            now = rest.astype(jnp.bfloat16).astype(jnp.float32)
            out = jnp.where(row == term, now, out)
            rest = rest - now
        norm_ref[...] = out.astype(jnp.bfloat16)


def adam(gradient, second_moment):
    rows, width = gradient.shape
    tile = 64
    return pl.pallas_call(
        adam_kernel,
        grid=(rows // tile,),
        in_specs=[pl.BlockSpec((tile, width), lambda i: (i, 0))] * 2,
        out_specs=[pl.BlockSpec((tile, width), lambda i: (i, 0)), pl.BlockSpec((16, 128), lambda i: (0, 0))],
        out_shape=[
            jax.ShapeDtypeStruct((rows, width), jnp.float32),
            jax.ShapeDtypeStruct((16, 128), jnp.bfloat16),
        ],
        scratch_shapes=[pltpu.VMEM((8, width), jnp.float32)],
        compiler_params=pltpu.CompilerParams(vmem_limit_bytes=56 * MIB),
        name="adam",
    )(gradient, second_moment)


RING = 4


def tables_kernel(rows_ref, cols_ref, owner_ref, place_ref, spread, fwd0, fwd1, back0, back1, from0, from1, offs, mine, far, row_of, owner_of):
    count = rows_ref.shape[1]
    devices, cols = row_of.shape
    me, group = place_ref[0], place_ref[1]
    for b in range(cols):
        for r in range(owner_of.shape[0]):
            owner_of[r, b] = 0
        for d in range(devices):
            row_of[d, b] = 0
        mine[0, b] = 0
        mine[1, b] = 0
        mine[2, b] = 0
    seen = jnp.int32(0)
    for k in range(count):
        r, b, o = rows_ref[group, k], cols_ref[group, k], owner_ref[group, k]
        row_of[o, b] = r
        owner_of[r, b] = o

        @pl.when(o == me)
        def _(r=r, b=b, seen=seen):
            mine[0, b] = seen
            mine[1, b] = 1
            mine[2, b] = r

        seen = seen + (o == me).astype(jnp.int32)

    c = me % 2
    y = (me // 2) % RING
    x = me // (2 * RING)
    yh, yl = y // 2, y % 2
    upper = c == 0
    sel = lambda a, b: jnp.where(upper, a, b)
    p_first, p_second = sel(x, y), sel(y, x)
    wrap = lambda v: (v + 2 * RING) % RING
    spread[0] = c
    sent = []
    for k, place in enumerate((2 * yh, 2 - 2 * yh, 2 * yh + 1, 3 - 2 * yh)):
        sent.append(sel(place, wrap(x + k)))
        spread[1 + k] = sent[k]
        spread[5 + k] = sel(place, wrap(x - k))
    for b, fwd in enumerate((fwd0, fwd1)):
        for flip in range(2):
            for k in range(RING):
                to = wrap(p_second + k)
                core = jnp.where(upper, flip, 1 - flip)
                row = row_of[sel((x * RING + to) * 2 + core, (to * RING + y) * 2 + core), b]
                for t in range(2):
                    n = (flip * RING + k) * 2 + t
                    inner = 2 * (row % 2) + t
                    fwd[0, n] = wrap(p_first - sel(row // 2, inner))
                    fwd[1, n] = sel(inner, row // 2)
    for b, (back, frm) in enumerate(((back0, from0), (back1, from1))):
        for k in range(RING):
            to = wrap(p_first + k)
            for u in range(4):
                owner = owner_of[sel(to * 2 + u // 2, u * 2 + to // 2), b]
                ox, oy, oc = owner // (2 * RING), (owner // 2) % RING, owner % 2
                back[0, k * 4 + u] = jnp.where(oc == c, 0, RING) + wrap(sel(oy, ox) - p_second)
                back[1, k * 4 + u] = sel(u % 2, to % 2)
        for k in range(4):
            owner = owner_of[sel(2 * x + sent[k] // 2, sent[k] * 2 + yh), b]
            ox, oy = owner // (2 * RING), (owner // 2) % RING
            frm[0, k] = wrap(p_first - sel(ox, oy))
            frm[1, k] = sent[k]
    for flip in range(2):
        from_upper = c == flip
        for k in range(RING):
            y_from, x_from = wrap(y - k), wrap(x - k)
            for t in range(2):
                for e in range(2):
                    up = ((y_from % 2) * 2 + e) * 256 + (y_from // 2) * 64 + t * 32
                    low = (t * 2 + e) * 256 + 128 + x_from * 32
                    offs[((flip * RING + k) * 2 + t) * 2 + e] = jnp.where(from_upper, up, low)
    for i, step in enumerate((0, 0, 3, 3, 1, 1, 2, 2)):
        far[0, i] = (group + step) % 4
        far[1, i] = c if i % 2 == 0 else 1 - c


def make_tables(rows, cols, owner, place, devices, col_count, row_count):
    i32 = lambda *shape: jax.ShapeDtypeStruct(shape, jnp.int32)
    shapes = [i32(9)] + [i32(2, 16)] * 4 + [i32(2, 4)] * 2 + [i32(32), i32(3, col_count), i32(2, 8)]
    shapes += [i32(devices, col_count), i32(row_count, col_count)]
    return pl.pallas_call(
        tables_kernel,
        in_specs=[SMEM] * 4,
        out_specs=[SMEM] * len(shapes),
        out_shape=shapes,
        name="tables",
    )(rows, cols, owner, place)


def stage_all(bufs, held, sems):
    copies = [pltpu.make_async_copy(src, held.at[i], sems.at[i]) for i, src in enumerate(bufs)]
    run_copies(copies)


def table_mover(name, table, ins, outs, pieces, piece_shape):
    n_in, n_out = len(ins), len(outs)

    def kernel(tab, *refs):
        srcs, dsts = refs[:n_in], refs[n_in : n_in + n_out]
        held, in_sem, out_sem = refs[n_in + n_out :]
        plan = pieces(tab, srcs, dsts)
        for i, (choices, _) in enumerate(plan):
            for cond, src in choices:
                copy = pltpu.make_async_copy(src, held.at[i], in_sem.at[i])
                if cond is None:
                    copy.start()
                else:
                    pl.when(cond)(copy.start)
        for i, (choices, dst) in enumerate(plan):
            pltpu.make_async_copy(choices[0][1], held.at[i], in_sem.at[i]).wait()
            pltpu.make_async_copy(held.at[i], dst, out_sem.at[i]).start()
        for i, (_, dst) in enumerate(plan):
            pltpu.make_async_copy(held.at[i], dst, out_sem.at[i]).wait()

    count = pieces.count
    size = 2 * count
    for d in piece_shape:
        size *= d
    return pl.pallas_call(
        kernel,
        in_specs=[SMEM] + [ANY] * n_in,
        out_specs=[ANY] * n_out,
        out_shape=[jax.ShapeDtypeStruct(o, jnp.bfloat16) for o in outs],
        scratch_shapes=[
            pltpu.VMEM((count, *piece_shape), jnp.bfloat16),
            pltpu.SemaphoreType.DMA((count,)),
            pltpu.SemaphoreType.DMA((count,)),
        ],
        compiler_params=pltpu.CompilerParams(vmem_limit_bytes=16 * MIB),
        cost_estimate=pl.CostEstimate(flops=0, bytes_accessed=2 * size, transcendentals=0),
        name=name,
    )(table, *ins)


def counted(count):
    def mark(f):
        f.count = count
        return f

    return mark


def picker(name, table, bufs, out_groups, outs_per, piece_shape, src_b=None, dst_b=None, before=()):
    n_in = len(bufs)
    per_buf = bufs[0].shape[0 if src_b is None else 1]

    def kernel(tab, *refs):
        srcs, dsts = refs[:n_in], refs[n_in + len(before) :][:out_groups]
        held, in_sem, out_sem = refs[n_in + len(before) + out_groups :]
        run_copies(
            [
                pltpu.make_async_copy(src if src_b is None else src.at[src_b], held.at[i], in_sem.at[i])
                for i, src in enumerate(srcs)
            ]
        )
        run_copies(
            [
                pltpu.make_async_copy(
                    held.at[tab[0, i * outs_per + j], tab[1, i * outs_per + j]],
                    dsts[i].at[j] if dst_b is None else dsts[i].at[dst_b, j],
                    out_sem.at[i * outs_per + j],
                )
                for i in range(out_groups)
                for j in range(outs_per)
            ]
        )

    size = 2
    for d in piece_shape:
        size *= d
    lead = () if dst_b is None else (2,)
    return pl.pallas_call(
        kernel,
        in_specs=[SMEM] + [ANY] * (n_in + len(before)),
        out_specs=[ANY] * out_groups,
        out_shape=[jax.ShapeDtypeStruct((*lead, outs_per, *piece_shape), jnp.bfloat16)] * out_groups,
        input_output_aliases={1 + n_in + i: i for i in range(len(before))},
        scratch_shapes=[
            pltpu.VMEM((n_in, per_buf, *piece_shape), jnp.bfloat16),
            pltpu.SemaphoreType.DMA((n_in,)),
            pltpu.SemaphoreType.DMA((out_groups * outs_per,)),
        ],
        compiler_params=pltpu.CompilerParams(vmem_limit_bytes=16 * MIB),
        cost_estimate=pl.CostEstimate(
            flops=0, bytes_accessed=size * (n_in * per_buf + out_groups * outs_per), transcendentals=0
        ),
        name=name,
    )(table, *bufs, *before)


def halves(v):
    hi = v.astype(jnp.bfloat16)
    return hi, (v - hi.astype(jnp.float32)).astype(jnp.bfloat16)


def column_copies(buf, box, to_box, sem):
    h, w = 64, 128
    depth, quarters = 4, 4
    made = []
    for k in range(quarters):
        for p in range(BS // w):
            away = buf.at[pl.ds(p * depth, depth), pl.ds(k * h, h), :]
            here = box.reshape(quarters, depth, h, BS).at[k, :, :, pl.ds(p * w, w)]
            n = k * (BS // w) + p
            made.append(pltpu.make_async_copy(*((away, here) if to_box else (here, away)), sem.at[n]))
    return made


def ring_copies(bufs, box, off_ref, to_box, sem):
    made = []
    for j, buf in enumerate(bufs):
        for t in range(2):
            for e in range(2):
                n = j * 4 + t * 2 + e
                here = box.at[pl.ds(pl.multiple_of(off_ref[n], 32), 32), :]
                away = buf.at[t, e]
                made.append(pltpu.make_async_copy(*((away, here) if to_box else (here, away)), sem.at[n]))
    return made


def shampoo_kernel(b, n_bufs, mine_ref, off_ref, norm_ref, left_ref, right_ref, *refs):
    ins, outs = refs[:n_bufs], refs[n_bufs : 2 * n_bufs]
    g, lv, rv, rhv, rlv, phv, plv, q, u, acc, norms, g_sem, root_sem, norm_sem, out_sem = refs[2 * n_bufs :]
    tile = 512
    tiles = BS // tile
    slot = mine_ref[0, b]

    def left_load(t):
        rows = pl.ds(pl.multiple_of(t * tile, tile), tile)
        return pltpu.make_async_copy(left_ref.at[0, 0, slot, rows, :], lv.at[rows, :], root_sem.at[t])

    def right_load(t):
        rows = pl.ds(pl.multiple_of(t * tile, tile), tile)
        return pltpu.make_async_copy(right_ref.at[0, 0, slot, rows, :], rv.at[rows, :], root_sem.at[tiles + t])

    def moves(bufs, box, to_box, sem):
        if n_bufs == 1:
            return column_copies(bufs[0], box, to_box, sem)
        return ring_copies(bufs, box, off_ref, to_box, sem)

    norm_load = pltpu.make_async_copy(norm_ref.at[:, pl.ds(256, 16), :], norms, norm_sem)
    dot = functools.partial(jnp.dot, preferred_element_type=jnp.float32)

    @pl.when(mine_ref[1, b] > 0)
    def _():
        grads = moves(ins, g, True, g_sem)
        left_load(0).start()
        for c in grads:
            c.start()
        for t in range(tiles):
            if t > 0:
                left_load(t).start()
            right_load(t).start()
        norm_load.start()
        for c in grads:
            c.wait()
        acc[...] = jnp.zeros_like(acc)

        def first(t, carry):
            rows = pl.ds(pl.multiple_of(t * tile, tile), tile)
            left_load(t).wait()
            right_load(t).wait()
            lh, ll = halves(lv[rows, :])
            rhv[rows, :], rlv[rows, :] = halves(rv[rows, :])
            phv[rows, :], plv[rows, :] = halves(dot(lh, g[...]) + dot(ll, g[...]))
            return carry

        def second(t, carry):
            rows = pl.ds(pl.multiple_of(t * tile, tile), tile)
            ph, plow = phv[rows, :], plv[rows, :]
            qt = dot(ph, rhv[...]) + (dot(ph, rlv[...]) + dot(plow, rhv[...]))
            q[rows, :] = qt
            acc[...] += jnp.sum((qt * qt).reshape(-1, 8, BS), axis=0)
            return carry

        lax.fori_loop(0, tiles, first, 0, unroll=True)
        lax.fori_loop(0, tiles, second, 0, unroll=True)
        norm_load.wait()
        device = lax.broadcasted_iota(jnp.int32, norms.shape, 0)
        lane = lax.broadcasted_iota(jnp.int32, norms.shape, 2)
        wanted = (device // 4 == mine_ref[2, b]) & (lane == b)
        adam_sq = jnp.sum(jnp.where(wanted, norms[...].astype(jnp.float32), 0.0))
        ratio = jnp.sqrt(adam_sq / (jnp.sum(acc[...]) + NORM_EPS))

        def scale(t, carry):
            rows = pl.ds(pl.multiple_of(t * 128, 128), 128)
            u[rows, :] = (ratio * q[rows, :]).astype(jnp.bfloat16)
            return carry

        lax.fori_loop(0, BS // 128, scale, 0)
        run_copies(moves(outs, u, False, out_sem))


def shampoo(b, mine, offsets, norms, left_root, right_root, bufs, out):
    big = (BS, BS)
    return pl.pallas_call(
        functools.partial(shampoo_kernel, b, len(bufs)),
        in_specs=[SMEM] * 2 + [ANY] * (3 + len(bufs)),
        out_specs=[ANY] * len(bufs),
        out_shape=[jax.ShapeDtypeStruct(out, jnp.bfloat16)] * len(bufs),
        scratch_shapes=[
            pltpu.VMEM(big, jnp.bfloat16),
            pltpu.VMEM(big, jnp.float32),
            pltpu.VMEM(big, jnp.float32),
            pltpu.VMEM(big, jnp.bfloat16),
            pltpu.VMEM(big, jnp.bfloat16),
            pltpu.VMEM(big, jnp.bfloat16),
            pltpu.VMEM(big, jnp.bfloat16),
            pltpu.VMEM(big, jnp.float32),
            pltpu.VMEM(big, jnp.bfloat16),
            pltpu.VMEM((8, BS), jnp.float32),
            pltpu.VMEM((norms.shape[0], 16, 128), jnp.bfloat16),
            pltpu.SemaphoreType.DMA((32,)),
            pltpu.SemaphoreType.DMA((8,)),
            pltpu.SemaphoreType.DMA,
            pltpu.SemaphoreType.DMA((32,)),
        ],
        compiler_params=pltpu.CompilerParams(vmem_limit_bytes=58 * MIB),
        cost_estimate=pl.CostEstimate(flops=10 * BS**3, bytes_accessed=12 * MIB, transcendentals=0),
        name="shampoo",
    )(mine, offsets, norms, left_root, right_root, *bufs)


def pick_kernel(b, row_ref, src, norm, dst, held, sent, in_sem, norm_sem, sem):
    owners, (_, h, _) = row_ref.shape[0], src.shape
    run_copies([pltpu.make_async_copy(src, held, in_sem), pltpu.make_async_copy(norm, sent, norm_sem)])
    run_copies(
        [
            pltpu.make_async_copy(held.at[row_ref[d, b]], dst.at[d, pl.ds(0, h), :], sem.at[0, d])
            for d in range(owners)
        ]
        + [pltpu.make_async_copy(sent, dst.at[d, pl.ds(h, sent.shape[0]), :], sem.at[1, d]) for d in range(owners)]
    )


def pick_for_owners(b, row_of, spread, norm):
    owners = row_of.shape[0]
    _, h, w = spread.shape
    return pl.pallas_call(
        functools.partial(pick_kernel, b),
        in_specs=[SMEM, ANY, ANY],
        out_specs=ANY,
        out_shape=jax.ShapeDtypeStruct((owners, h + norm.shape[0], w), jnp.bfloat16),
        scratch_shapes=[
            pltpu.VMEM(spread.shape, jnp.bfloat16),
            pltpu.VMEM(norm.shape, jnp.bfloat16),
            pltpu.SemaphoreType.DMA,
            pltpu.SemaphoreType.DMA,
            pltpu.SemaphoreType.DMA((2, owners)),
        ],
        compiler_params=pltpu.CompilerParams(vmem_limit_bytes=16 * MIB),
        cost_estimate=pl.CostEstimate(flops=0, bytes_accessed=3 * MIB, transcendentals=0),
        name="pick_for_owners",
    )(row_of, spread, norm)


def unpick_kernel(b, owner_ref, src, dst, held, sem, out_sem):
    rows = owner_ref.shape[0]
    run_copies([pltpu.make_async_copy(src.at[owner_ref[r, b]], held.at[r], sem.at[r]) for r in range(rows)])
    run_copies([pltpu.make_async_copy(held, dst, out_sem)])


def pick_from_owners(b, owner_of, got):
    shape = (owner_of.shape[0], *got.shape[1:])
    return pl.pallas_call(
        functools.partial(unpick_kernel, b),
        in_specs=[SMEM, ANY],
        out_specs=ANY,
        out_shape=jax.ShapeDtypeStruct(shape, jnp.bfloat16),
        scratch_shapes=[
            pltpu.VMEM(shape, jnp.bfloat16),
            pltpu.SemaphoreType.DMA((shape[0],)),
            pltpu.SemaphoreType.DMA,
        ],
        compiler_params=pltpu.CompilerParams(vmem_limit_bytes=16 * MIB),
        cost_estimate=pl.CostEstimate(flops=0, bytes_accessed=1 * MIB, transcendentals=0),
        name="pick_from_owners",
    )(owner_of, got)


def column_rows_kernel(b, cols, tab, own, before, after, far_lo, far_hi, out, held, sem, out_sem):
    parts, h, w = own.shape
    sides = BS // w
    depth = parts // sides
    copies = []
    for k, src in enumerate((own, before, after)):
        for p in range(sides):
            copies.append((src.at[pl.ds(p * depth, depth)], held.at[k, :, :, pl.ds(p * w, w)]))
    for half, src in enumerate((far_lo, far_hi)):
        for p in range(sides // 2):
            lanes = pl.ds((half * (sides // 2) + p) * w, w)
            copies.append((src.at[pl.ds(p * depth, depth)], held.at[3, :, :, lanes]))
    run_copies([pltpu.make_async_copy(s, d, sem.at[n]) for n, (s, d) in enumerate(copies)])
    puts = []
    for k, i in enumerate((0, 2, 4, 6)):
        col = pl.multiple_of(tab[0, i] * (cols * BS) + b * BS, BS)
        puts.append(
            pltpu.make_async_copy(held.at[k].reshape(depth * h, BS), out.at[:, pl.ds(col, BS)], out_sem.at[k])
        )
    run_copies(puts)


def column_rows(b, cols, groups, table, bufs):
    parts, h, w = bufs[0].shape
    depth = parts * w // BS
    return pl.pallas_call(
        functools.partial(column_rows_kernel, b, cols),
        in_specs=[SMEM] + [ANY] * 5,
        out_specs=ANY,
        out_shape=jax.ShapeDtypeStruct((depth * h, groups * cols * BS), jnp.bfloat16),
        scratch_shapes=[
            pltpu.VMEM((4, depth, h, BS), jnp.bfloat16),
            pltpu.SemaphoreType.DMA((4 * BS // w,)),
            pltpu.SemaphoreType.DMA((4,)),
        ],
        compiler_params=pltpu.CompilerParams(vmem_limit_bytes=16 * MIB),
        cost_estimate=pl.CostEstimate(flops=0, bytes_accessed=4 * MIB, transcendentals=0),
        name="column_rows",
    )(table, *bufs)


def rows_kernel(b, cols, tab, *refs):
    ins, out = refs[:8], refs[-4]
    held, in_sem, out_sem = refs[-3:]
    h = ins[0].shape[0]
    copies = [pltpu.make_async_copy(src, held.at[i], in_sem.at[i]) for i, src in enumerate(ins)]
    for c in copies:
        c.start()
    puts = []
    for i in range(8):
        row = pl.multiple_of(tab[1, i] * h, h)
        col = pl.multiple_of(tab[0, i] * (cols * BS) + b * BS, BS)
        copies[i].wait()
        put = pltpu.make_async_copy(held.at[i], out.at[pl.ds(row, h), pl.ds(col, BS)], out_sem.at[i])
        put.start()
        puts.append(put)
    for put in puts:
        put.wait()


def whole_rows(b, cols, groups, table, bufs, before):
    h = bufs[0].shape[0]
    shape = jax.ShapeDtypeStruct((2 * h, groups * cols * BS), jnp.bfloat16)
    extra = [] if before is None else [before]
    return pl.pallas_call(
        functools.partial(rows_kernel, b, cols),
        in_specs=[SMEM] + [ANY] * (8 + len(extra)),
        out_specs=ANY,
        out_shape=shape,
        input_output_aliases={9: 0} if extra else {},
        scratch_shapes=[
            pltpu.VMEM((8, h, BS), jnp.bfloat16),
            pltpu.SemaphoreType.DMA((8,)),
            pltpu.SemaphoreType.DMA((8,)),
        ],
        compiler_params=pltpu.CompilerParams(vmem_limit_bytes=16 * MIB),
        cost_estimate=pl.CostEstimate(flops=0, bytes_accessed=4 * MIB, transcendentals=0),
        name="whole_rows",
    )(table, *bufs, *extra)


def permute(value, move):
    pairs = []
    for x in range(RING):
        for y in range(RING):
            for c in range(2):
                to = move(x, y, c)
                if to is not None:
                    tx, ty, tc = to
                    pairs.append(((x * RING + y) * 2 + c, ((tx % RING) * RING + ty % RING) * 2 + tc))
    return lax.ppermute(value, "fsdp", pairs)


def swap_cores(value):
    return permute(value, lambda x, y, c: (x, y, 1 - c))


def along_first(value, k):
    return permute(value, lambda x, y, c: (x + k, y, c) if c == 0 else (x, y + k, c))


def along_second(value, k, flip):
    return permute(value, lambda x, y, c: (x, y + k, c ^ flip) if c == 0 else (x + k, y, c ^ flip))


def back_second(value, k, flip):
    return permute(value, lambda x, y, c: (x, y - k, c ^ flip) if c ^ flip == 0 else (x - k, y, c ^ flip))


def spread_move(value, k):
    return permute(value, lambda x, y, c: (x + k, y, c) if c == 1 else ((x, y + 2, c) if k != 2 else None))


def on_device(gradient, second_moment, left_root, right_root, block_rows, block_cols, block_owner):
    shard_rows, width = gradient.shape
    cols = width // BS
    fsdp = lax.axis_size("fsdp")
    groups = lax.axis_size("group")
    me = lax.axis_index("fsdp")
    group = lax.axis_index("group")
    quarters = BS // shard_rows
    row_count = fsdp // quarters
    half = shard_rows // 2
    part = half // 4
    place = jnp.stack([me, group]).astype(jnp.int32)
    up = [(i, (i + 1) % groups) for i in range(groups)]
    down = [(i, (i - 1) % groups) for i in range(groups)]
    across = lambda v, w: lax.ppermute(v, "group", w)
    every = lambda v: lax.all_to_all(v, "fsdp", 0, 0, tiled=True)

    h, w = 64, 128
    mixed = gradient[:, :BS].reshape(shard_rows // h, h, BS // w, w).transpose(2, 0, 1, 3)
    spread = every(mixed.reshape(fsdp, h, w))

    give = lax.dynamic_slice(gradient, ((1 - me % 2) * half, BS), (half, BS))
    other = swap_cores(give)
    moment, norm = adam(gradient, second_moment)
    tables = make_tables(block_rows, block_cols, block_owner, place, fsdp, cols, row_count)
    spread_tab, _, fwd, _, back_tab, _, from_tab, offsets, mine, far_tab, row_of, owner_of = tables

    lanes = pl.ds(BS, BS)

    @counted(6)
    def spread_pieces(tab, ins, outs):
        mine_ref, other_ref = ins
        core = tab[0]
        made = []
        for k in (1, 2, 3):
            at = pl.multiple_of(tab[1 + k] * part, part)
            here = pl.multiple_of(core * half + at, part)
            made.append(([(None, mine_ref.at[pl.ds(here, part), lanes])], outs[k - 1].at[core]))
            made.append(([(None, other_ref.at[pl.ds(at, part), :])], outs[k - 1].at[1 - core]))
        return made

    sends = table_mover("spread_send", spread_tab, [gradient, other], [(2, part, BS)] * 3, spread_pieces, (part, BS))
    arrived = {k: spread_move(sends[k - 1], k) for k in (1, 3, 2)}
    arrived = [arrived[k] for k in (1, 2, 3)]

    @counted(8)
    def stack_pieces(tab, ins, outs):
        mine_ref, other_ref, got = ins[0], ins[1], ins[2:]
        core = tab[0]
        made = []
        for k in range(4):
            u = tab[5 + k]
            at = pl.multiple_of(tab[5 + k] * part, part)
            here = pl.multiple_of(core * half + at, part)
            local = (mine_ref.at[pl.ds(here, part), lanes], other_ref.at[pl.ds(at, part), :])
            for e in range(2):
                src_e = core if e == 0 else 1 - core
                if k == 0:
                    choices = [(None, local[e])]
                elif k == 2:
                    choices = [(core == 0, local[e]), (core == 1, got[1].at[src_e])]
                else:
                    choices = [(None, got[k - 1].at[src_e])]
                made.append((choices, outs[0].at[u, src_e]))
        return made

    (stacked,) = table_mover(
        "spread_stack", spread_tab, [gradient, other, *arrived], [(4, 2, part, BS)], stack_pieces, (part, BS)
    )
    stacked, spread = lax.optimization_barrier((stacked, spread))

    picked0 = pick_for_owners(0, row_of, spread.reshape(row_count, quarters * h, w), norm)
    got = {k: along_first(stacked, k) for k in (1, 3, 2)}
    picked0, got = lax.optimization_barrier((picked0, got))
    got0 = every(picked0)
    picked = picker("to_owners", fwd, [stacked, got[1], got[2], got[3]], 8, 2, (2, part, BS))
    far_pieces = [(0, 1), (0, 3), (1, 1), (1, 3), (0, 2), (1, 2), (1, 0)]
    bufs = {(0, 0): picked[0]}
    for f, k in far_pieces:
        bufs[f, k] = along_second(picked[f * 4 + k], k, f)

    got0, picked_first = lax.optimization_barrier((got0, picked[7]))
    (done0,) = shampoo(0, mine, offsets, got0, left_root, right_root, [got0], (fsdp, quarters * h, w))
    bufs = [bufs[f, k] for f in range(2) for k in range(4)]
    done0, bufs = lax.optimization_barrier((done0, bufs))
    done = shampoo(1, mine, offsets, got0, left_root, right_root, bufs, bufs[0].shape)

    home0 = every(pick_from_owners(0, owner_of, every(done0)).reshape(fsdp, h, w))
    before, after = across(home0, up), across(home0, down)
    far_lo, far_hi = across(before[: fsdp // 2], up), across(after[fsdp // 2 :], down)
    update = column_rows(0, cols, groups, far_tab, [home0, before, after, far_lo, far_hi])

    back = {(0, 0): done[0]}
    for f, k in far_pieces:
        back[f, k] = back_second(done[f * 4 + k], k, f)
    back = [back[f, k] for f in range(2) for k in range(4)]
    replies = picker("to_homes", back_tab, back, 4, 4, (2, part, BS))
    held = {k: along_first(replies[k], k) for k in (1, 3, 2)}
    held = [replies[0]] + [held[k] for k in (1, 2, 3)]
    slots = picker("from_owners", from_tab, held, 4, 1, (2, part, BS))
    arrived = [spread_move(slots[k][0], k) for k in (1, 2, 3)]

    @counted(8)
    def home_pieces(tab, ins, outs):
        core = tab[0]
        made = []
        for k in range(4):
            at = pl.multiple_of(tab[5 + k] * part, part)
            for i, e in enumerate((core, 1 - core)):
                if k == 2:
                    choices = [(core == 0, ins[1].at[0, e]), (core == 1, ins[3].at[e])]
                elif k == 0:
                    choices = [(None, ins[0].at[0, e])]
                else:
                    choices = [(None, ins[1 + k].at[e])]
                made.append((choices, outs[i].at[pl.ds(at, part), :]))
        return made

    keep, give = table_mover(
        "home", spread_tab, [slots[0], slots[2], *arrived], [(half, BS)] * 2, home_pieces, (part, BS)
    )
    got = swap_cores(give)
    k_up, k_down, g_up, g_down = across(keep, up), across(keep, down), across(got, up), across(got, down)
    k_far, g_far = across(k_up, up), across(g_down, down)
    update = whole_rows(
        1, cols, groups, far_tab, [keep, got, k_up, g_up, k_down, g_down, k_far, g_far], update
    )
    return update, moment


def solution(mesh):
    placed = (
        P("fsdp", "group"),
        P("fsdp", "group"),
        P("group", "fsdp", None, None, None),
        P("group", "fsdp", None, None, None),
        P(),
        P(),
        P(),
    )
    return jax.shard_map(
        on_device,
        mesh=mesh,
        in_specs=placed,
        out_specs=(P("fsdp", None), P("fsdp", "group")),
        check_vma=False,
    )
```

```python
import functools

import jax
import jax.numpy as jnp
from jax import lax
from jax.experimental import pallas as pl
from jax.experimental.pallas import tpu as pltpu
from jax.sharding import PartitionSpec as P

BS = 1024
BETA_TWO = 0.999
ADAM_EPS = 1e-08
NORM_EPS = 1e-06

ANY = pl.BlockSpec(memory_space=pl.ANY)
SMEM = pl.BlockSpec(memory_space=pltpu.SMEM)
MIB = 1 << 20


def run_copies(copies):
    for c in copies:
        c.start()
    for c in copies:
        c.wait()


def adam_kernel(g_ref, m_ref, mo_ref, norm_ref, acc):
    step, cols = pl.program_id(0), acc.shape[1] // BS

    @pl.when(step == 0)
    def _():
        acc[...] = jnp.zeros_like(acc)

    g = g_ref[...].astype(jnp.float32)
    moment = BETA_TWO * m_ref[...] + (1.0 - BETA_TWO) * g * g
    mo_ref[...] = moment
    adam = g / (jnp.sqrt(moment) + ADAM_EPS)
    acc[...] += jnp.sum((adam * adam).reshape(-1, 8, acc.shape[1]), axis=0)

    @pl.when(step == pl.num_programs(0) - 1)
    def _():
        row = lax.broadcasted_iota(jnp.int32, norm_ref.shape, 0)
        lane = lax.broadcasted_iota(jnp.int32, norm_ref.shape, 1)
        rest = jnp.zeros(norm_ref.shape, jnp.float32)
        for b in range(cols):
            rest = jnp.where(lane == b, jnp.sum(acc[:, b * BS : (b + 1) * BS]), rest)
        out = jnp.zeros(norm_ref.shape, jnp.float32)
        for term in range(3):
            now = rest.astype(jnp.bfloat16).astype(jnp.float32)
            out = jnp.where(row == term, now, out)
            rest = rest - now
        norm_ref[...] = out.astype(jnp.bfloat16)


def adam(gradient, second_moment):
    rows, width = gradient.shape
    tile = 64
    return pl.pallas_call(
        adam_kernel,
        grid=(rows // tile,),
        in_specs=[pl.BlockSpec((tile, width), lambda i: (i, 0))] * 2,
        out_specs=[pl.BlockSpec((tile, width), lambda i: (i, 0)), pl.BlockSpec((16, 128), lambda i: (0, 0))],
        out_shape=[
            jax.ShapeDtypeStruct((rows, width), jnp.float32),
            jax.ShapeDtypeStruct((16, 128), jnp.bfloat16),
        ],
        scratch_shapes=[pltpu.VMEM((8, width), jnp.float32)],
        compiler_params=pltpu.CompilerParams(vmem_limit_bytes=56 * MIB),
        name="adam",
    )(gradient, second_moment)


RING = 4


def tables_kernel(rows_ref, cols_ref, owner_ref, place_ref, spread, fwd0, fwd1, back0, back1, from0, from1, offs, mine, far, row_of, owner_of):
    count = rows_ref.shape[1]
    devices, cols = row_of.shape
    me, group = place_ref[0], place_ref[1]
    for b in range(cols):
        for r in range(owner_of.shape[0]):
            owner_of[r, b] = 0
        for d in range(devices):
            row_of[d, b] = 0
        mine[0, b] = 0
        mine[1, b] = 0
        mine[2, b] = 0
    seen = jnp.int32(0)
    for k in range(count):
        r, b, o = rows_ref[group, k], cols_ref[group, k], owner_ref[group, k]
        row_of[o, b] = r
        owner_of[r, b] = o

        @pl.when(o == me)
        def _(r=r, b=b, seen=seen):
            mine[0, b] = seen
            mine[1, b] = 1
            mine[2, b] = r

        seen = seen + (o == me).astype(jnp.int32)

    c = me % 2
    y = (me // 2) % RING
    x = me // (2 * RING)
    yh, yl = y // 2, y % 2
    upper = c == 0
    sel = lambda a, b: jnp.where(upper, a, b)
    p_first, p_second = sel(x, y), sel(y, x)
    wrap = lambda v: (v + 2 * RING) % RING
    spread[0] = c
    sent = []
    for k, place in enumerate((2 * yh, 2 - 2 * yh, 2 * yh + 1, 3 - 2 * yh)):
        sent.append(sel(place, wrap(x + k)))
        spread[1 + k] = sent[k]
        spread[5 + k] = sel(place, wrap(x - k))
    for b, fwd in enumerate((fwd0, fwd1)):
        for flip in range(2):
            for k in range(RING):
                to = wrap(p_second + k)
                core = jnp.where(upper, flip, 1 - flip)
                row = row_of[sel((x * RING + to) * 2 + core, (to * RING + y) * 2 + core), b]
                for t in range(2):
                    n = (flip * RING + k) * 2 + t
                    inner = 2 * (row % 2) + t
                    fwd[0, n] = wrap(p_first - sel(row // 2, inner))
                    fwd[1, n] = sel(inner, row // 2)
    for b, (back, frm) in enumerate(((back0, from0), (back1, from1))):
        for k in range(RING):
            to = wrap(p_first + k)
            for u in range(4):
                owner = owner_of[sel(to * 2 + u // 2, u * 2 + to // 2), b]
                ox, oy, oc = owner // (2 * RING), (owner // 2) % RING, owner % 2
                back[0, k * 4 + u] = jnp.where(oc == c, 0, RING) + wrap(sel(oy, ox) - p_second)
                back[1, k * 4 + u] = sel(u % 2, to % 2)
        for k in range(4):
            owner = owner_of[sel(2 * x + sent[k] // 2, sent[k] * 2 + yh), b]
            ox, oy = owner // (2 * RING), (owner // 2) % RING
            frm[0, k] = wrap(p_first - sel(ox, oy))
            frm[1, k] = sent[k]
    for flip in range(2):
        from_upper = c == flip
        for k in range(RING):
            y_from, x_from = wrap(y - k), wrap(x - k)
            for t in range(2):
                for e in range(2):
                    up = ((y_from % 2) * 2 + e) * 256 + (y_from // 2) * 64 + t * 32
                    low = (t * 2 + e) * 256 + 128 + x_from * 32
                    offs[((flip * RING + k) * 2 + t) * 2 + e] = jnp.where(from_upper, up, low)
    for i, step in enumerate((0, 0, 3, 3, 1, 1, 2, 2)):
        far[0, i] = (group + step) % 4
        far[1, i] = c if i % 2 == 0 else 1 - c


def make_tables(rows, cols, owner, place, devices, col_count, row_count):
    i32 = lambda *shape: jax.ShapeDtypeStruct(shape, jnp.int32)
    shapes = [i32(9)] + [i32(2, 16)] * 4 + [i32(2, 4)] * 2 + [i32(32), i32(3, col_count), i32(2, 8)]
    shapes += [i32(devices, col_count), i32(row_count, col_count)]
    return pl.pallas_call(
        tables_kernel,
        in_specs=[SMEM] * 4,
        out_specs=[SMEM] * len(shapes),
        out_shape=shapes,
        name="tables",
    )(rows, cols, owner, place)


def stage_all(bufs, held, sems):
    copies = [pltpu.make_async_copy(src, held.at[i], sems.at[i]) for i, src in enumerate(bufs)]
    run_copies(copies)


def table_mover(name, table, ins, outs, pieces, piece_shape):
    n_in, n_out = len(ins), len(outs)

    def kernel(tab, *refs):
        srcs, dsts = refs[:n_in], refs[n_in : n_in + n_out]
        held, in_sem, out_sem = refs[n_in + n_out :]
        plan = pieces(tab, srcs, dsts)
        for i, (choices, _) in enumerate(plan):
            for cond, src in choices:
                copy = pltpu.make_async_copy(src, held.at[i], in_sem.at[i])
                if cond is None:
                    copy.start()
                else:
                    pl.when(cond)(copy.start)
        for i, (choices, dst) in enumerate(plan):
            pltpu.make_async_copy(choices[0][1], held.at[i], in_sem.at[i]).wait()
            pltpu.make_async_copy(held.at[i], dst, out_sem.at[i]).start()
        for i, (_, dst) in enumerate(plan):
            pltpu.make_async_copy(held.at[i], dst, out_sem.at[i]).wait()

    count = pieces.count
    size = 2 * count
    for d in piece_shape:
        size *= d
    return pl.pallas_call(
        kernel,
        in_specs=[SMEM] + [ANY] * n_in,
        out_specs=[ANY] * n_out,
        out_shape=[jax.ShapeDtypeStruct(o, jnp.bfloat16) for o in outs],
        scratch_shapes=[
            pltpu.VMEM((count, *piece_shape), jnp.bfloat16),
            pltpu.SemaphoreType.DMA((count,)),
            pltpu.SemaphoreType.DMA((count,)),
        ],
        compiler_params=pltpu.CompilerParams(vmem_limit_bytes=16 * MIB),
        cost_estimate=pl.CostEstimate(flops=0, bytes_accessed=2 * size, transcendentals=0),
        name=name,
    )(table, *ins)


def counted(count):
    def mark(f):
        f.count = count
        return f

    return mark


def picker(name, table, bufs, out_groups, outs_per, piece_shape, src_b=None, dst_b=None, before=()):
    n_in = len(bufs)
    per_buf = bufs[0].shape[0 if src_b is None else 1]

    def kernel(tab, *refs):
        srcs, dsts = refs[:n_in], refs[n_in + len(before) :][:out_groups]
        held, in_sem, out_sem = refs[n_in + len(before) + out_groups :]
        run_copies(
            [
                pltpu.make_async_copy(src if src_b is None else src.at[src_b], held.at[i], in_sem.at[i])
                for i, src in enumerate(srcs)
            ]
        )
        run_copies(
            [
                pltpu.make_async_copy(
                    held.at[tab[0, i * outs_per + j], tab[1, i * outs_per + j]],
                    dsts[i].at[j] if dst_b is None else dsts[i].at[dst_b, j],
                    out_sem.at[i * outs_per + j],
                )
                for i in range(out_groups)
                for j in range(outs_per)
            ]
        )

    size = 2
    for d in piece_shape:
        size *= d
    lead = () if dst_b is None else (2,)
    return pl.pallas_call(
        kernel,
        in_specs=[SMEM] + [ANY] * (n_in + len(before)),
        out_specs=[ANY] * out_groups,
        out_shape=[jax.ShapeDtypeStruct((*lead, outs_per, *piece_shape), jnp.bfloat16)] * out_groups,
        input_output_aliases={1 + n_in + i: i for i in range(len(before))},
        scratch_shapes=[
            pltpu.VMEM((n_in, per_buf, *piece_shape), jnp.bfloat16),
            pltpu.SemaphoreType.DMA((n_in,)),
            pltpu.SemaphoreType.DMA((out_groups * outs_per,)),
        ],
        compiler_params=pltpu.CompilerParams(vmem_limit_bytes=16 * MIB),
        cost_estimate=pl.CostEstimate(
            flops=0, bytes_accessed=size * (n_in * per_buf + out_groups * outs_per), transcendentals=0
        ),
        name=name,
    )(table, *bufs, *before)


def halves(v):
    hi = v.astype(jnp.bfloat16)
    return hi, (v - hi.astype(jnp.float32)).astype(jnp.bfloat16)


def column_copies(buf, box, to_box, sem):
    h, w = 64, 128
    depth, quarters = 4, 4
    made = []
    for k in range(quarters):
        for p in range(BS // w):
            away = buf.at[pl.ds(p * depth, depth), pl.ds(k * h, h), :]
            here = box.reshape(quarters, depth, h, BS).at[k, :, :, pl.ds(p * w, w)]
            n = k * (BS // w) + p
            made.append(pltpu.make_async_copy(*((away, here) if to_box else (here, away)), sem.at[n]))
    return made


def ring_copies(bufs, box, off_ref, to_box, sem):
    made = []
    for j, buf in enumerate(bufs):
        for t in range(2):
            for e in range(2):
                n = j * 4 + t * 2 + e
                here = box.at[pl.ds(pl.multiple_of(off_ref[n], 32), 32), :]
                away = buf.at[t, e]
                made.append(pltpu.make_async_copy(*((away, here) if to_box else (here, away)), sem.at[n]))
    return made


def shampoo_kernel(b, n_bufs, mine_ref, off_ref, norm_ref, left_ref, right_ref, *refs):
    ins, outs = refs[:n_bufs], refs[n_bufs : 2 * n_bufs]
    g, lv, rv, rhv, rlv, phv, plv, q, u, acc, norms, g_sem, root_sem, norm_sem, out_sem = refs[2 * n_bufs :]
    tile = 512
    tiles = BS // tile
    slot = mine_ref[0, b]

    def left_load(t):
        rows = pl.ds(pl.multiple_of(t * tile, tile), tile)
        return pltpu.make_async_copy(left_ref.at[0, 0, slot, rows, :], lv.at[rows, :], root_sem.at[t])

    def right_load(t):
        rows = pl.ds(pl.multiple_of(t * tile, tile), tile)
        return pltpu.make_async_copy(right_ref.at[0, 0, slot, rows, :], rv.at[rows, :], root_sem.at[tiles + t])

    def moves(bufs, box, to_box, sem):
        if n_bufs == 1:
            return column_copies(bufs[0], box, to_box, sem)
        return ring_copies(bufs, box, off_ref, to_box, sem)

    norm_load = pltpu.make_async_copy(norm_ref.at[:, pl.ds(256, 16), :], norms, norm_sem)
    dot = functools.partial(jnp.dot, preferred_element_type=jnp.float32)

    @pl.when(mine_ref[1, b] > 0)
    def _():
        grads = moves(ins, g, True, g_sem)
        left_load(0).start()
        for c in grads:
            c.start()
        for t in range(tiles):
            if t > 0:
                left_load(t).start()
            right_load(t).start()
        norm_load.start()
        for c in grads:
            c.wait()
        acc[...] = jnp.zeros_like(acc)

        def first(t, carry):
            rows = pl.ds(pl.multiple_of(t * tile, tile), tile)
            left_load(t).wait()
            right_load(t).wait()
            lh, ll = halves(lv[rows, :])
            rhv[rows, :], rlv[rows, :] = halves(rv[rows, :])
            phv[rows, :], plv[rows, :] = halves(dot(lh, g[...]) + dot(ll, g[...]))
            return carry

        def second(t, carry):
            rows = pl.ds(pl.multiple_of(t * tile, tile), tile)
            ph, plow = phv[rows, :], plv[rows, :]
            qt = dot(ph, rhv[...]) + (dot(ph, rlv[...]) + dot(plow, rhv[...]))
            q[rows, :] = qt
            acc[...] += jnp.sum((qt * qt).reshape(-1, 8, BS), axis=0)
            return carry

        lax.fori_loop(0, tiles, first, 0, unroll=True)
        lax.fori_loop(0, tiles, second, 0, unroll=True)
        norm_load.wait()
        device = lax.broadcasted_iota(jnp.int32, norms.shape, 0)
        lane = lax.broadcasted_iota(jnp.int32, norms.shape, 2)
        wanted = (device // 4 == mine_ref[2, b]) & (lane == b)
        adam_sq = jnp.sum(jnp.where(wanted, norms[...].astype(jnp.float32), 0.0))
        ratio = jnp.sqrt(adam_sq / (jnp.sum(acc[...]) + NORM_EPS))

        def scale(t, carry):
            rows = pl.ds(pl.multiple_of(t * 128, 128), 128)
            u[rows, :] = (ratio * q[rows, :]).astype(jnp.bfloat16)
            return carry

        lax.fori_loop(0, BS // 128, scale, 0)
        run_copies(moves(outs, u, False, out_sem))


def shampoo(b, mine, offsets, norms, left_root, right_root, bufs, out):
    big = (BS, BS)
    return pl.pallas_call(
        functools.partial(shampoo_kernel, b, len(bufs)),
        in_specs=[SMEM] * 2 + [ANY] * (3 + len(bufs)),
        out_specs=[ANY] * len(bufs),
        out_shape=[jax.ShapeDtypeStruct(out, jnp.bfloat16)] * len(bufs),
        scratch_shapes=[
            pltpu.VMEM(big, jnp.bfloat16),
            pltpu.VMEM(big, jnp.float32),
            pltpu.VMEM(big, jnp.float32),
            pltpu.VMEM(big, jnp.bfloat16),
            pltpu.VMEM(big, jnp.bfloat16),
            pltpu.VMEM(big, jnp.bfloat16),
            pltpu.VMEM(big, jnp.bfloat16),
            pltpu.VMEM(big, jnp.float32),
            pltpu.VMEM(big, jnp.bfloat16),
            pltpu.VMEM((8, BS), jnp.float32),
            pltpu.VMEM((norms.shape[0], 16, 128), jnp.bfloat16),
            pltpu.SemaphoreType.DMA((32,)),
            pltpu.SemaphoreType.DMA((8,)),
            pltpu.SemaphoreType.DMA,
            pltpu.SemaphoreType.DMA((32,)),
        ],
        compiler_params=pltpu.CompilerParams(vmem_limit_bytes=58 * MIB),
        cost_estimate=pl.CostEstimate(flops=10 * BS**3, bytes_accessed=12 * MIB, transcendentals=0),
        name="shampoo",
    )(mine, offsets, norms, left_root, right_root, *bufs)


def pick_kernel(b, row_ref, src, norm, dst, held, sent, in_sem, norm_sem, sem):
    owners, (_, h, _) = row_ref.shape[0], src.shape
    run_copies([pltpu.make_async_copy(src, held, in_sem), pltpu.make_async_copy(norm, sent, norm_sem)])
    run_copies(
        [
            pltpu.make_async_copy(held.at[row_ref[d, b]], dst.at[d, pl.ds(0, h), :], sem.at[0, d])
            for d in range(owners)
        ]
        + [pltpu.make_async_copy(sent, dst.at[d, pl.ds(h, sent.shape[0]), :], sem.at[1, d]) for d in range(owners)]
    )


def pick_for_owners(b, row_of, spread, norm):
    owners = row_of.shape[0]
    _, h, w = spread.shape
    return pl.pallas_call(
        functools.partial(pick_kernel, b),
        in_specs=[SMEM, ANY, ANY],
        out_specs=ANY,
        out_shape=jax.ShapeDtypeStruct((owners, h + norm.shape[0], w), jnp.bfloat16),
        scratch_shapes=[
            pltpu.VMEM(spread.shape, jnp.bfloat16),
            pltpu.VMEM(norm.shape, jnp.bfloat16),
            pltpu.SemaphoreType.DMA,
            pltpu.SemaphoreType.DMA,
            pltpu.SemaphoreType.DMA((2, owners)),
        ],
        compiler_params=pltpu.CompilerParams(vmem_limit_bytes=16 * MIB),
        cost_estimate=pl.CostEstimate(flops=0, bytes_accessed=3 * MIB, transcendentals=0),
        name="pick_for_owners",
    )(row_of, spread, norm)


def unpick_kernel(b, owner_ref, src, dst, held, sem, out_sem):
    rows = owner_ref.shape[0]
    run_copies([pltpu.make_async_copy(src.at[owner_ref[r, b]], held.at[r], sem.at[r]) for r in range(rows)])
    run_copies([pltpu.make_async_copy(held, dst, out_sem)])


def pick_from_owners(b, owner_of, got):
    shape = (owner_of.shape[0], *got.shape[1:])
    return pl.pallas_call(
        functools.partial(unpick_kernel, b),
        in_specs=[SMEM, ANY],
        out_specs=ANY,
        out_shape=jax.ShapeDtypeStruct(shape, jnp.bfloat16),
        scratch_shapes=[
            pltpu.VMEM(shape, jnp.bfloat16),
            pltpu.SemaphoreType.DMA((shape[0],)),
            pltpu.SemaphoreType.DMA,
        ],
        compiler_params=pltpu.CompilerParams(vmem_limit_bytes=16 * MIB),
        cost_estimate=pl.CostEstimate(flops=0, bytes_accessed=1 * MIB, transcendentals=0),
        name="pick_from_owners",
    )(owner_of, got)


def column_rows_kernel(b, cols, tab, own, before, after, far_lo, far_hi, out, held, sem, out_sem):
    parts, h, w = own.shape
    sides = BS // w
    depth = parts // sides
    copies = []
    for k, src in enumerate((own, before, after)):
        for p in range(sides):
            copies.append((src.at[pl.ds(p * depth, depth)], held.at[k, :, :, pl.ds(p * w, w)]))
    for half, src in enumerate((far_lo, far_hi)):
        for p in range(sides // 2):
            lanes = pl.ds((half * (sides // 2) + p) * w, w)
            copies.append((src.at[pl.ds(p * depth, depth)], held.at[3, :, :, lanes]))
    run_copies([pltpu.make_async_copy(s, d, sem.at[n]) for n, (s, d) in enumerate(copies)])
    puts = []
    for k, i in enumerate((0, 2, 4, 6)):
        col = pl.multiple_of(tab[0, i] * (cols * BS) + b * BS, BS)
        puts.append(
            pltpu.make_async_copy(held.at[k].reshape(depth * h, BS), out.at[:, pl.ds(col, BS)], out_sem.at[k])
        )
    run_copies(puts)


def column_rows(b, cols, groups, table, bufs):
    parts, h, w = bufs[0].shape
    depth = parts * w // BS
    return pl.pallas_call(
        functools.partial(column_rows_kernel, b, cols),
        in_specs=[SMEM] + [ANY] * 5,
        out_specs=ANY,
        out_shape=jax.ShapeDtypeStruct((depth * h, groups * cols * BS), jnp.bfloat16),
        scratch_shapes=[
            pltpu.VMEM((4, depth, h, BS), jnp.bfloat16),
            pltpu.SemaphoreType.DMA((4 * BS // w,)),
            pltpu.SemaphoreType.DMA((4,)),
        ],
        compiler_params=pltpu.CompilerParams(vmem_limit_bytes=16 * MIB),
        cost_estimate=pl.CostEstimate(flops=0, bytes_accessed=4 * MIB, transcendentals=0),
        name="column_rows",
    )(table, *bufs)


def rows_kernel(b, cols, tab, *refs):
    ins, out = refs[:8], refs[-4]
    held, in_sem, out_sem = refs[-3:]
    h = ins[0].shape[0]
    copies = [pltpu.make_async_copy(src, held.at[i], in_sem.at[i]) for i, src in enumerate(ins)]
    for c in copies:
        c.start()
    puts = []
    for i in range(8):
        row = pl.multiple_of(tab[1, i] * h, h)
        col = pl.multiple_of(tab[0, i] * (cols * BS) + b * BS, BS)
        copies[i].wait()
        put = pltpu.make_async_copy(held.at[i], out.at[pl.ds(row, h), pl.ds(col, BS)], out_sem.at[i])
        put.start()
        puts.append(put)
    for put in puts:
        put.wait()


def whole_rows(b, cols, groups, table, bufs, before):
    h = bufs[0].shape[0]
    shape = jax.ShapeDtypeStruct((2 * h, groups * cols * BS), jnp.bfloat16)
    extra = [] if before is None else [before]
    return pl.pallas_call(
        functools.partial(rows_kernel, b, cols),
        in_specs=[SMEM] + [ANY] * (8 + len(extra)),
        out_specs=ANY,
        out_shape=shape,
        input_output_aliases={9: 0} if extra else {},
        scratch_shapes=[
            pltpu.VMEM((8, h, BS), jnp.bfloat16),
            pltpu.SemaphoreType.DMA((8,)),
            pltpu.SemaphoreType.DMA((8,)),
        ],
        compiler_params=pltpu.CompilerParams(vmem_limit_bytes=16 * MIB),
        cost_estimate=pl.CostEstimate(flops=0, bytes_accessed=4 * MIB, transcendentals=0),
        name="whole_rows",
    )(table, *bufs, *extra)


def permute(value, move):
    pairs = []
    for x in range(RING):
        for y in range(RING):
            for c in range(2):
                to = move(x, y, c)
                if to is not None:
                    tx, ty, tc = to
                    pairs.append(((x * RING + y) * 2 + c, ((tx % RING) * RING + ty % RING) * 2 + tc))
    return lax.ppermute(value, "fsdp", pairs)


def swap_cores(value):
    return permute(value, lambda x, y, c: (x, y, 1 - c))


def along_first(value, k):
    return permute(value, lambda x, y, c: (x + k, y, c) if c == 0 else (x, y + k, c))


def along_second(value, k, flip):
    return permute(value, lambda x, y, c: (x, y + k, c ^ flip) if c == 0 else (x + k, y, c ^ flip))


def back_second(value, k, flip):
    return permute(value, lambda x, y, c: (x, y - k, c ^ flip) if c ^ flip == 0 else (x - k, y, c ^ flip))


def spread_move(value, k):
    return permute(value, lambda x, y, c: (x + k, y, c) if c == 1 else ((x, y + 2, c) if k != 2 else None))


def on_device(gradient, second_moment, left_root, right_root, block_rows, block_cols, block_owner):
    shard_rows, width = gradient.shape
    cols = width // BS
    fsdp = lax.axis_size("fsdp")
    groups = lax.axis_size("group")
    me = lax.axis_index("fsdp")
    group = lax.axis_index("group")
    quarters = BS // shard_rows
    row_count = fsdp // quarters
    half = shard_rows // 2
    part = half // 4
    place = jnp.stack([me, group]).astype(jnp.int32)
    up = [(i, (i + 1) % groups) for i in range(groups)]
    down = [(i, (i - 1) % groups) for i in range(groups)]
    across = lambda v, w: lax.ppermute(v, "group", w)
    every = lambda v: lax.all_to_all(v, "fsdp", 0, 0, tiled=True)

    h, w = 64, 128
    mixed = gradient[:, :BS].reshape(shard_rows // h, h, BS // w, w).transpose(2, 0, 1, 3)
    spread = every(mixed.reshape(fsdp, h, w))

    give = lax.dynamic_slice(gradient, ((1 - me % 2) * half, BS), (half, BS))
    other = swap_cores(give)
    moment, norm = adam(gradient, second_moment)
    tables = make_tables(block_rows, block_cols, block_owner, place, fsdp, cols, row_count)
    spread_tab, _, fwd, _, back_tab, _, from_tab, offsets, mine, far_tab, row_of, owner_of = tables

    lanes = pl.ds(BS, BS)

    @counted(6)
    def spread_pieces(tab, ins, outs):
        mine_ref, other_ref = ins
        core = tab[0]
        made = []
        for k in (1, 2, 3):
            at = pl.multiple_of(tab[1 + k] * part, part)
            here = pl.multiple_of(core * half + at, part)
            made.append(([(None, mine_ref.at[pl.ds(here, part), lanes])], outs[k - 1].at[core]))
            made.append(([(None, other_ref.at[pl.ds(at, part), :])], outs[k - 1].at[1 - core]))
        return made

    sends = table_mover("spread_send", spread_tab, [gradient, other], [(2, part, BS)] * 3, spread_pieces, (part, BS))
    arrived = {k: spread_move(sends[k - 1], k) for k in (1, 3, 2)}
    arrived = [arrived[k] for k in (1, 2, 3)]

    @counted(8)
    def stack_pieces(tab, ins, outs):
        mine_ref, other_ref, got = ins[0], ins[1], ins[2:]
        core = tab[0]
        made = []
        for k in range(4):
            u = tab[5 + k]
            at = pl.multiple_of(tab[5 + k] * part, part)
            here = pl.multiple_of(core * half + at, part)
            local = (mine_ref.at[pl.ds(here, part), lanes], other_ref.at[pl.ds(at, part), :])
            for e in range(2):
                src_e = core if e == 0 else 1 - core
                if k == 0:
                    choices = [(None, local[e])]
                elif k == 2:
                    choices = [(core == 0, local[e]), (core == 1, got[1].at[src_e])]
                else:
                    choices = [(None, got[k - 1].at[src_e])]
                made.append((choices, outs[0].at[u, src_e]))
        return made

    (stacked,) = table_mover(
        "spread_stack", spread_tab, [gradient, other, *arrived], [(4, 2, part, BS)], stack_pieces, (part, BS)
    )
    stacked, spread = lax.optimization_barrier((stacked, spread))

    picked0 = pick_for_owners(0, row_of, spread.reshape(row_count, quarters * h, w), norm)
    got = {k: along_first(stacked, k) for k in (1, 3, 2)}
    picked0, got = lax.optimization_barrier((picked0, got))
    got0 = every(picked0)
    picked = picker("to_owners", fwd, [stacked, got[1], got[2], got[3]], 8, 2, (2, part, BS))
    picked = list(picked)
    far_pieces = [(0, 1), (0, 3), (1, 1), (1, 3), (0, 2), (1, 2)]
    bufs = {(0, 0): picked[0]}
    bufs[1, 0] = along_second(picked[4], 0, 1)
    picked[2], picked[6], bufs[1, 0] = lax.optimization_barrier((picked[2], picked[6], bufs[1, 0]))
    for f, k in far_pieces:
        bufs[f, k] = along_second(picked[f * 4 + k], k, f)

    got0, picked_first = lax.optimization_barrier((got0, picked[7]))
    (done0,) = shampoo(0, mine, offsets, got0, left_root, right_root, [got0], (fsdp, quarters * h, w))
    bufs = [bufs[f, k] for f in range(2) for k in range(4)]
    done0, bufs = lax.optimization_barrier((done0, bufs))
    done = shampoo(1, mine, offsets, got0, left_root, right_root, bufs, bufs[0].shape)

    home0 = every(pick_from_owners(0, owner_of, every(done0)).reshape(fsdp, h, w))
    before, after = across(home0, up), across(home0, down)
    far_lo, far_hi = across(before[: fsdp // 2], up), across(after[fsdp // 2 :], down)
    update = column_rows(0, cols, groups, far_tab, [home0, before, after, far_lo, far_hi])

    back = {(0, 0): done[0]}
    done = list(done)
    back[1, 0] = back_second(done[4], 0, 1)
    done[2], done[6], back[1, 0] = lax.optimization_barrier((done[2], done[6], back[1, 0]))
    for f, k in far_pieces:
        back[f, k] = back_second(done[f * 4 + k], k, f)
    back = [back[f, k] for f in range(2) for k in range(4)]
    replies = picker("to_homes", back_tab, back, 4, 4, (2, part, BS))
    held = {k: along_first(replies[k], k) for k in (1, 3, 2)}
    held = [replies[0]] + [held[k] for k in (1, 2, 3)]
    slots = picker("from_owners", from_tab, held, 4, 1, (2, part, BS))
    arrived = [spread_move(slots[k][0], k) for k in (1, 2, 3)]

    @counted(8)
    def home_pieces(tab, ins, outs):
        core = tab[0]
        made = []
        for k in range(4):
            at = pl.multiple_of(tab[5 + k] * part, part)
            for i, e in enumerate((core, 1 - core)):
                if k == 2:
                    choices = [(core == 0, ins[1].at[0, e]), (core == 1, ins[3].at[e])]
                elif k == 0:
                    choices = [(None, ins[0].at[0, e])]
                else:
                    choices = [(None, ins[1 + k].at[e])]
                made.append((choices, outs[i].at[pl.ds(at, part), :]))
        return made

    keep, give = table_mover(
        "home", spread_tab, [slots[0], slots[2], *arrived], [(half, BS)] * 2, home_pieces, (part, BS)
    )
    got = swap_cores(give)
    k_up, k_down, g_up, g_down = across(keep, up), across(keep, down), across(got, up), across(got, down)
    k_far, g_far = across(k_up, up), across(g_down, down)
    update = whole_rows(
        1, cols, groups, far_tab, [keep, got, k_up, g_up, k_down, g_down, k_far, g_far], update
    )
    return update, moment


def solution(mesh):
    placed = (
        P("fsdp", "group"),
        P("fsdp", "group"),
        P("group", "fsdp", None, None, None),
        P("group", "fsdp", None, None, None),
        P(),
        P(),
        P(),
    )
    return jax.shard_map(
        on_device,
        mesh=mesh,
        in_specs=placed,
        out_specs=(P("fsdp", None), P("fsdp", "group")),
        check_vma=False,
    )
```
